256 devices in a mesh: row: 16 (over x, y), col: 16 (over z, core).
Axes of the slice: x: 4, y: 4, z: 8, core: 2. Of those that a mesh axis runs over, the one named last changes fastest.
Arguments:
- inducing_desc: bfloat16 [2, 1960, 2048], P(None, None, 'row'), may hold values from -0.8984375 to 0.8984375
- candidate_desc: bfloat16 [1960, 12288], P(None, 'col'), may hold values from -0.8984375 to 0.8984375
- first_inverse: float32 [2048, 2048], P('row', 'col'), may hold values from -2 to 2, as said below
- coupling: float32 [2048, 2048], P('row', 'col'), may hold values from -0.0625 to 0.0625
- second_inverse: float32 [2048, 2048], P('row', 'col'), may hold values from -2 to 2, as said below
Outputs:
- first_solved: float32 [2048, 12288], P('row', 'col')
- second_solved: float32 [2048, 12288], P('row', 'col')
- explained: float32 [12288], P('col')
The draws below stay inside these ranges and needn't reach their ends.
Inputs may be any that keep to these rules, and one draw needn't show every extreme that they name: `first_inverse`: lower triangular: zero above the diagonal, positive on it. `second_inverse`: lower triangular: zero above the diagonal, positive on it.
All inputs are finite; a program needn't handle non-finite values.
Results may differ from the reference program's by a relative error of at most 0.0003.
Values may be sent and summed in bfloat16 or wider, within the bound.
A program may use at most 128 MiB of HBM per device.

```python
import jax
import jax.numpy as jnp
from jax import lax

W = 1960
B = 2048
CANDS = 12288


def assemble_block(rough, base):
    index = jnp.arange(B)
    lower = jnp.where(index[:, None] > index[None, :], jnp.clip(rough, -6.0, 6.0) * (0.6 / jnp.sqrt(B * 1.0)), 0.0)
    diagonal = base * (1.0 + 0.75 * index.astype(jnp.float32) / B)
    return (lower + jnp.diag(diagonal)).astype(jnp.float32)


def draw_first_inverse(key, part):
    key = jax.random.fold_in(key, 11)
    key_rough, key_base = jax.random.split(key)
    rough = jax.random.normal(key_rough, (B, B), jnp.float32)
    base = jnp.exp(jax.random.uniform(key_base, (B,), jnp.float32, -0.6931472, 0.0))
    return assemble_block(rough, base)


def draw_second_inverse(key, part):
    key = jax.random.fold_in(key, 23)
    key_rough, key_base = jax.random.split(key)
    rough = jax.random.normal(key_rough, (B, B), jnp.float32)
    base = jnp.exp(jax.random.uniform(key_base, (B,), jnp.float32, -0.6931472, 0.0))
    return assemble_block(rough, base)


def levels(key, extent, cuts, smallest, largest):
    level = 1.0
    for position, parts in cuts:
        steps = jax.random.uniform(jax.random.fold_in(jax.random.fold_in(key, 6), position), (parts,), jnp.float32, smallest / len(cuts), largest / len(cuts))
        level = level * jnp.repeat(jnp.exp(steps), extent[position] // parts).reshape((-1,) + (1,) * (len(extent) - 1 - position))
    return level


def normal_values(stream_key, dims, spread, reach, cuts=(), dtype=jnp.bfloat16):
    array = jax.random.normal(stream_key, dims, jnp.float32) * spread
    if len(cuts) > 0:
        array = levels(stream_key, dims, cuts, -0.22, 0.18) * array
    return jnp.clip(array, min=-reach, max=reach).astype(dtype)


def setup_inputs(seed: int = 0) -> dict:
    arg_keys = jax.random.split(jax.random.key(seed), 6)
    inducing_desc = normal_values(arg_keys[0], (2, W, B), (W ** -0.25), 0.8984375, ((2, 16),))
    candidate_desc = normal_values(arg_keys[1], (W, CANDS), (W ** -0.25), 0.8984375, ((1, 16),))
    first_inverse = draw_first_inverse(jax.random.fold_in(arg_keys[5], 71), 0)
    coupling = normal_values(arg_keys[3], (B, B), (4 * B) ** -0.5, 0.0625, ((0, 16), (1, 16)), jnp.float32)
    second_inverse = draw_second_inverse(jax.random.fold_in(arg_keys[5], 71), 0)
    return dict(inducing_desc=inducing_desc, candidate_desc=candidate_desc, first_inverse=first_inverse, coupling=coupling, second_inverse=second_inverse)


def kernel_columns(inducing, candidates):
    inner = lax.dot_general(inducing, candidates, (((0,), (0,)), ((), ())), preferred_element_type=jnp.float32)
    return inner * inner


def product(left, right):
    return jnp.dot(left, right, precision=lax.Precision.HIGHEST, preferred_element_type=jnp.float32)


def reference(inducing_desc, candidate_desc, first_inverse, coupling, second_inverse):
    first_kernel = kernel_columns(inducing_desc[0], candidate_desc)
    second_kernel = kernel_columns(inducing_desc[1], candidate_desc)
    first_solved = product(first_inverse, first_kernel)
    remainder = second_kernel - product(coupling, first_solved)
    second_solved = product(second_inverse, remainder)
    total = jnp.sum(first_solved * first_solved, axis=0) + jnp.sum(second_solved * second_solved, axis=0)
    explained = total / (2.0 * B)
    return first_solved, second_solved, explained
```

```python
import jax
import jax.numpy as jnp
from jax import lax
from jax.experimental import pallas as pl
from jax.experimental.pallas import tpu as pltpu
from jax.sharding import PartitionSpec as P

W = 1960
B = 2048
CH = 128
Q = 6
PAIR = 2 * CH
MESH = pl.DeviceIdType.MESH
F32 = jnp.float32
BF16 = jnp.bfloat16

N_SEND = 640


def split(v):
    hi = v.astype(BF16)
    lo = (v - hi.astype(F32)).astype(BF16)
    return hi, lo


class Sent:
    def __init__(self, copy, number):
        self.copy = copy
        self.number = number


def task_order():
    tasks = []
    period, step = 13.0, 2.1
    base = 3.0
    for n in range(3):
        for q in range(Q):
            t = base + n * period + q * step
            if n == 0:
                t = base + q * 0.9
            for name, dt in (("b", 2.4), ("c", 4.6), ("d", 6.6), ("e", 9.0)):
                tt = t + dt
                if n == 0 and name in "cde":
                    tt = 10.0 + q * step + (dt - 4.6)
                tasks.append((tt, name, n, q))
    for k in range(5):
        tasks.append((2.0 + 1.9 * k, "ring", 0, k))
        tasks.append((8.4 + 2.2 * k, "ring", 1, k))
        tasks.append((18.5 + 2.4 * k, "ring", 2, k))
    tasks.append((9.9, "fac", 0, 0))
    tasks.append((17.8, "fac", 1, 0))
    tasks.append((28.9, "fac", 2, 0))
    for p in range(Q // 2):
        tasks.append((2.5 + 0.5 * p, "k1", 0, p))
        tasks.append((4.5 + 1.7 * p, "k2", 0, p))
    tasks.sort()
    return tasks


def kernel(desc_hbm, cand_hbm, f_hbm, c_hbm, s_hbm, first_out, second_out, ex_out,
           desc, cand, fin, fsend, fbuf, gbuf, pbuf, r1, r2, k2, esum, ebuf, lsem, ssem, rsem):
    row = lax.axis_index("row")
    col = lax.axis_index("col")
    x, y = row // 4, row % 4
    z, core = col // 2, col % 2
    counter = [0]
    sent = []

    def at(r, c):
        return {"row": r, "col": c}

    x_right, x_left = at(((x + 1) % 4) * 4 + y, col), at(((x + 3) % 4) * 4 + y, col)
    y_right, y_left = at(x * 4 + (y + 1) % 4, col), at(x * 4 + (y + 3) % 4, col)
    z_right, z_left = at(row, ((z + 1) % 8) * 2 + core), at(row, ((z + 7) % 8) * 2 + core)
    sibling = at(row, z * 2 + 1 - core)

    to_y = 2 * (z % 2) + core
    to_z = jnp.where(y < 2, z, z + 1 - 2 * (z % 2))
    from_z = (z // 2) * 2 + y // 2
    from_col = from_z * 2 + y % 2
    other_parity = (z % 2 + y // 2) % 2

    def new(src, dst, device):
        k = counter[0]
        counter[0] += 1
        return pltpu.make_async_remote_copy(
            src_ref=src, dst_ref=dst, send_sem=ssem.at[k], recv_sem=rsem.at[k],
            device_id=device, device_id_type=MESH)

    def send(src, dst, device):
        copy = new(src, dst, device)
        copy.start()
        sent.append(copy)
        return Sent(copy, counter[0] - 1)

    loads = []
    for m, ref in enumerate((f_hbm, c_hbm, s_hbm)):
        loads.append(pltpu.make_async_copy(ref, fin.at[m], lsem.at[m]))
    loads.append(pltpu.make_async_copy(desc_hbm, desc, lsem.at[3]))
    for p in range(Q // 2):
        columns = pl.ds(p * PAIR, PAIR)
        loads.append(pltpu.make_async_copy(cand_hbm.at[:, columns], cand.at[:, columns], lsem.at[4 + p]))
    for copy in loads:
        copy.start()

    barrier = pltpu.get_barrier_semaphore()
    partners = [at((row + d) % 16, col) for d in range(1, 16)] + [z_right, z_left, sibling]
    for i in range(2):
        partners.append(at(x * 4 + to_y, to_z * 2 + i))
        partners.append(at(x * 4 + 2 * other_parity + i, from_col))
    for device in partners:
        pl.semaphore_signal(barrier, inc=1, device_id=device, device_id_type=MESH)
    pl.semaphore_wait(barrier, len(partners))

    for m in range(3):
        loads[m].wait()
        hi, lo = split(fin[m])
        fsend[m, 0] = hi
        fsend[m, 1] = lo

    def rows_of(yi):
        return pl.ds(pl.multiple_of(yi * 128, 128), 128)

    def columns_of(zo):
        return pl.ds(pl.multiple_of((zo // 2) * 128, 128), 128)

    groups = ((0, 1), (1, 1), (2, 1))
    exchange = {}
    mine = (to_y == y) & (to_z == z)
    for g, (m0, count) in enumerate(groups):
        ms = pl.ds(m0, count)
        spot = (rows_of(y), columns_of(z))
        for c in range(2):
            k = counter[0]
            counter[0] += 2
            copy = pltpu.make_async_remote_copy(
                src_ref=fsend.at[ms, c], dst_ref=fbuf.at[ms, c, spot[0], spot[1]],
                send_sem=ssem.at[k], recv_sem=rsem.at[k + y % 2],
                device_id=at(x * 4 + to_y, to_z * 2 + c), device_id_type=MESH)
            local = mine & (core == c)
            exchange[g, c] = (copy, local, k)

            @pl.when(jnp.logical_not(local))
            def _(copy=copy):
                copy.start()

            @pl.when(local)
            def _(m0=m0, count=count, c=c, spot=spot):
                for m in range(m0, m0 + count):
                    fbuf[m, c, spot[0], spot[1]] = fsend[m, c]

    def wait_exchange(g):
        m0, count = groups[g]
        ms = pl.ds(m0, count)
        for c in range(2):
            _, _, k = exchange[g, c]
            for i in range(2):
                yi = 2 * other_parity + i
                local = (yi == y) & (from_col == col)
                spot = fbuf.at[ms, c, rows_of(yi), columns_of(z)]
                arrival = pltpu.make_async_remote_copy(
                    src_ref=spot, dst_ref=spot, send_sem=ssem.at[k], recv_sem=rsem.at[k + i],
                    device_id=sibling, device_id_type=MESH)

                @pl.when((core == c) & jnp.logical_not(local))
                def _(arrival=arrival):
                    arrival.wait_recv()

    def piece(g, h, zo, half=None):
        m0, count = groups[g]
        other = (zo % 2 + y // 2) % 2
        start, size = other * 256, 256
        if half is not None:
            start, size = start + half * 128, 128
        return fbuf.at[pl.ds(m0, count), h, pl.ds(pl.multiple_of(start, 128), size), columns_of(zo)]

    ring_sends = {}
    sibling_sends = {0: [], 1: [], 2: []}

    def ring(g, k):
        h = core
        right_zo, left_zo = (z + 8 - k) % 8, (z + k) % 8
        if k == 0:
            wait_exchange(g)
            own = piece(g, h, z)
            ring_sends[g, 1] = (send(own, own, z_right), send(own, own, z_left))
            sibling_sends[g].append((send(own, own, sibling), z, None))
            return
        for side, zo in ((0, right_zo), (1, left_zo)):
            half = None if k < 4 else side
            got = piece(g, h, zo, half)
            arrival = ring_sends[g, k][side]
            pltpu.make_async_remote_copy(
                src_ref=got, dst_ref=got, send_sem=ssem.at[arrival.number], recv_sem=rsem.at[arrival.number],
                device_id=sibling, device_id_type=MESH).wait_recv()
            if k < 4:
                out = got if k < 3 else piece(g, h, zo, side)
                onward = send(out, out, z_right if side == 0 else z_left)
                ring_sends.setdefault((g, k + 1), []).append(onward)
            sibling_sends[g].append((send(got, got, sibling), zo, half))

    def factors_ready(g):
        for copy, zo, half in sibling_sends[g]:
            got = piece(g, 1 - core, zo, half)
            pltpu.make_async_remote_copy(
                src_ref=got, dst_ref=got, send_sem=ssem.at[copy.number], recv_sem=rsem.at[copy.number],
                device_id=sibling, device_id_type=MESH).wait_recv()

    def block_of(i):
        return pl.ds(pl.multiple_of((i % 4) * 128, 128), 128)

    def half_of(i, half):
        return pl.ds(pl.multiple_of((i % 4) * 128 + half * 64, 64), 64)

    def wait_recv(copy, ref):
        pltpu.make_async_remote_copy(
            src_ref=ref, dst_ref=ref, send_sem=ssem.at[copy.number], recv_sem=rsem.at[copy.number],
            device_id=sibling, device_id_type=MESH).wait_recv()

    state = {}

    def put(n, q, v):
        hi, lo = split(v)
        gbuf[n, q, block_of(x), 0:CH] = hi
        gbuf[n, q, block_of(x), CH:PAIR] = lo
        own = gbuf.at[n, q, block_of(x)]
        state["a", n, q] = (send(own, own, x_right), send(own, own, x_left))

    def kernel_columns(panel, p):
        inner = lax.dot_general(
            desc[panel], cand[:, p * PAIR:(p + 1) * PAIR], (((0,), (0,)), ((), ())),
            preferred_element_type=F32)
        return inner * inner

    def k1_task(p):
        if p == 0:
            loads[3].wait()
        loads[4 + p].wait()
        value = kernel_columns(0, p)
        for i in range(2):
            put(0, 2 * p + i, value[:, i * CH:(i + 1) * CH])

    def k2_task(p):
        value = kernel_columns(1, p)
        for i in range(2):
            k2[2 * p + i] = value[:, i * CH:(i + 1) * CH]

    def b_task(n, q):
        to_right, to_left = state["a", n, q]
        wait_recv(to_right, gbuf.at[n, q, block_of(x + 3)])
        top = gbuf.at[n, q, half_of(x + 3, 0)]
        on_right = send(top, top, x_right)
        wait_recv(to_left, gbuf.at[n, q, block_of(x + 1)])
        bottom = gbuf.at[n, q, half_of(x + 1, 1)]
        on_left = send(bottom, bottom, x_left)
        state["b", n, q] = (on_right, on_left)

    def c_task(n, q):
        on_right, on_left = state["b", n, q]
        wait_recv(on_right, gbuf.at[n, q, half_of(x + 2, 0)])
        wait_recv(on_left, gbuf.at[n, q, half_of(x + 2, 1)])
        v = gbuf[n, q]
        v_hi = v[:, 0:CH]
        for i in range(2):
            rows = slice(i * 256, (i + 1) * 256)
            both = jnp.dot(fbuf[n, 0, rows, :], v, preferred_element_type=F32)
            low = jnp.dot(fbuf[n, 1, rows, :], v_hi, preferred_element_type=F32)
            pbuf[n, q, rows, :] = both[:, 0:CH] + (both[:, CH:PAIR] + low)
        copies = (
            send(pbuf.at[n, q, half_of(y + 2, 0)], r1.at[n, q, 0], y_right),
            send(pbuf.at[n, q, half_of(y + 2, 1)], r1.at[n, q, 1], y_left),
            send(pbuf.at[n, q, half_of(y + 1, 1)], r2.at[n, q, 0, pl.ds(64, 64)], y_right),
            send(pbuf.at[n, q, half_of(y + 3, 0)], r2.at[n, q, 1, pl.ds(0, 64)], y_left),
        )
        state["c", n, q] = copies

    def d_task(n, q):
        copies = state["c", n, q]
        wait_recv(copies[0], r1.at[n, q, 0])
        rows = half_of(y + 1, 0)
        pbuf[n, q, rows, :] = pbuf[n, q, rows, :] + r1[n, q, 0]
        right = send(pbuf.at[n, q, rows], r2.at[n, q, 0, pl.ds(0, 64)], y_right)
        wait_recv(copies[1], r1.at[n, q, 1])
        rows = half_of(y + 3, 1)
        pbuf[n, q, rows, :] = pbuf[n, q, rows, :] + r1[n, q, 1]
        left = send(pbuf.at[n, q, rows], r2.at[n, q, 1, pl.ds(64, 64)], y_left)
        state["d", n, q] = (right, left)

    def e_task(n, q):
        copies = state["c", n, q]
        right, left = state["d", n, q]
        wait_recv(copies[2], r2.at[n, q, 0, pl.ds(64, 64)])
        wait_recv(copies[3], r2.at[n, q, 1, pl.ds(0, 64)])
        wait_recv(right, r2.at[n, q, 0, pl.ds(0, 64)])
        wait_recv(left, r2.at[n, q, 1, pl.ds(64, 64)])
        value = pbuf[n, q, block_of(y), :] + (r2[n, q, 0] + r2[n, q, 1])
        columns = slice(q * CH, (q + 1) * CH)
        if n == 0:
            put(1, q, value)
            first_out[:, columns] = value
            esum[q:q + 1, :] = jnp.sum(value * value, axis=0, keepdims=True)
        elif n == 1:
            put(2, q, k2[q] - value)
        else:
            esum[q:q + 1, :] = esum[q:q + 1, :] + jnp.sum(value * value, axis=0, keepdims=True)
            second_out[:, columns] = value

    esum[...] = jnp.zeros_like(esum)
    for _, name, n, q in task_order():
        if name == "ring":
            ring(n, q)
        elif name == "fac":
            factors_ready(n)
        elif name == "k1":
            k1_task(q)
        elif name == "k2":
            k2_task(q)
        else:
            {"b": b_task, "c": c_task, "d": d_task, "e": e_task}[name](n, q)

    ebuf[pl.ds(row, 1)] = esum[...][None]
    spread = []
    for d in range(1, 16):
        spread.append(send(esum, ebuf.at[row], at((row + d) % 16, col)))
    for d in range(1, 16):
        wait_recv(spread[d - 1], ebuf.at[(row + 16 - d) % 16])
    total = ebuf[0]
    for i in range(1, 16):
        total = total + ebuf[i]
    ex_out[...] = total * (1.0 / (2.0 * B))

    for copy in sent:
        copy.wait_send()
    for copy, local, _ in exchange.values():
        @pl.when(jnp.logical_not(local))
        def _(copy=copy):
            copy.wait_send()
    assert counter[0] <= N_SEND


def shards(inducing_desc, candidate_desc, first_inverse, coupling, second_inverse):
    hbm = pl.BlockSpec(memory_space=pl.ANY)
    vmem = pl.BlockSpec(memory_space=pltpu.VMEM)
    first, second, explained = pl.pallas_call(
        kernel,
        out_shape=(
            jax.ShapeDtypeStruct((128, Q * CH), F32),
            jax.ShapeDtypeStruct((128, Q * CH), F32),
            jax.ShapeDtypeStruct((8, 128), F32),
        ),
        in_specs=[hbm] * 5,
        out_specs=(vmem, vmem, vmem),
        scratch_shapes=[
            pltpu.VMEM((2, W, 128), BF16),
            pltpu.VMEM((W, Q * CH), BF16),
            pltpu.VMEM((3, 128, 128), F32),
            pltpu.VMEM((3, 2, 128, 128), BF16),
            pltpu.VMEM((3, 2, 512, 512), BF16),
            pltpu.VMEM((3, Q, 512, PAIR), BF16),
            pltpu.VMEM((3, Q, 512, CH), F32),
            pltpu.VMEM((3, Q, 2, 64, CH), F32),
            pltpu.VMEM((3, Q, 2, 128, CH), F32),
            pltpu.VMEM((Q, 128, CH), F32),
            pltpu.VMEM((8, 128), F32),
            pltpu.VMEM((16, 8, 128), F32),
            pltpu.SemaphoreType.DMA((4 + Q // 2,)),
            pltpu.SemaphoreType.DMA((N_SEND,)),
            pltpu.SemaphoreType.DMA((N_SEND,)),
        ],
        compiler_params=pltpu.CompilerParams(
            collective_id=0, has_side_effects=True, vmem_limit_bytes=48 * 1024 * 1024),
    )(inducing_desc, candidate_desc, first_inverse, coupling, second_inverse)
    return first, second, explained[:Q].reshape(Q * CH)


def solution(mesh):
    return jax.shard_map(
        shards,
        mesh=mesh,
        in_specs=(
            P(None, None, "row"),
            P(None, "col"),
            P("row", "col"),
            P("row", "col"),
            P("row", "col"),
        ),
        out_specs=(P("row", "col"), P("row", "col"), P("col")),
        check_vma=False,
    )
```

```python
import jax
import jax.numpy as jnp
from jax import lax
from jax.experimental import pallas as pl
from jax.experimental.pallas import tpu as pltpu
from jax.sharding import PartitionSpec as P

W = 1960
B = 2048
CH = 128
Q = 6
PAIR = 2 * CH
MESH = pl.DeviceIdType.MESH
F32 = jnp.float32
BF16 = jnp.bfloat16

N_SEND = 256
ROWS = 144
TINY = 1e-35


def split(v):
    hi = v.astype(BF16)
    lo = (v - hi.astype(F32)).astype(BF16)
    return hi, lo


def encode(ref, v, diagonal=None):
    top = jnp.max(jnp.abs(v), axis=0, keepdims=True)
    s = (top * 1.01 + TINY).astype(BF16)
    t = jnp.abs(v) * (250.0 / s.astype(F32))
    e = jnp.floor(t)
    c = jnp.exp2(e - 125.0) * ((t - e) + 1.0)
    ref[0:128, :] = jnp.where(v < 0.0, -c, c).astype(BF16)
    tail = jnp.broadcast_to(s.astype(F32), (16, 128))
    if diagonal is not None:
        hi, lo = split(diagonal)
        index = lax.broadcasted_iota(jnp.int32, (16, 128), 0)
        tail = jnp.where(index == 1, hi.astype(F32), jnp.where(index == 2, lo.astype(F32), tail))
    ref[128:144, :] = tail.astype(BF16)


def decode(ref):
    c = ref[0:128, :].astype(F32)
    tail = ref[128:144, :].astype(F32)
    a = jnp.abs(c)
    e = jnp.floor(jnp.log2(a) + 0.002)
    t = (e + (a * jnp.exp2(-e) + 124.0)) * (tail[0:1, :] * (1.0 / 250.0))
    return jnp.where(c < 0.0, -t, t), tail[1:2, :] + tail[2:3, :]


class Sent:
    def __init__(self, copy, number):
        self.copy = copy
        self.number = number


def task_order():
    tasks = []
    start, period, step, flight = 14.0, 10.6, 1.65, 5.2
    for n in range(3):
        for q in range(Q):
            t = start + n * period + q * step
            tasks.append((t, "c", n, q))
            tasks.append((t + flight, "e", n, q))
    for p in range(Q // 2):
        tasks.append((3.0 + 0.5 * p, "k1", 0, p))
        tasks.append((5.0 + 0.5 * p, "k2", 0, p))
    for m in range(3):
        tasks.append(((2.0, 7.0, 13.0)[m], "fsend", m, 0))
        tasks.append(((10.0, 16.0, 24.0)[m], "sibling", m, 0))
        tasks.append(((13.9, 20.0, 30.0)[m], "fac", m, 0))
    tasks.sort()
    return tasks


def kernel(desc_hbm, cand_hbm, f_hbm, c_hbm, s_hbm, first_out, second_out, ex_out,
           desc, cand, fin, fmsg, frecv, fbuf, vown, vsend, vrecv, gbuf, pown, ptmp, psend, precv,
           k2, esum, ebuf, lsem, ssem, rsem):
    row = lax.axis_index("row")
    col = lax.axis_index("col")
    x, y = row // 4, row % 4
    z, core = col // 2, col % 2
    counter = [0]
    sent = []

    def at(r, c):
        return {"row": r, "col": c}

    sibling = at(row, z * 2 + 1 - core)
    to_y = 2 * (z % 2) + core
    parity = y % 2

    def take(count=1):
        k = counter[0]
        counter[0] += count
        return k

    def send(src, dst, device):
        k = take()
        copy = pltpu.make_async_remote_copy(
            src_ref=src, dst_ref=dst, send_sem=ssem.at[k], recv_sem=rsem.at[k],
            device_id=device, device_id_type=MESH)
        copy.start()
        sent.append(copy)
        return k

    def arrival(k, ref):
        return pltpu.make_async_remote_copy(
            src_ref=ref, dst_ref=ref, send_sem=ssem.at[k], recv_sem=rsem.at[k],
            device_id=sibling, device_id_type=MESH)

    loads = []
    for m, ref in enumerate((f_hbm, c_hbm, s_hbm)):
        loads.append(pltpu.make_async_copy(ref, fin.at[m], lsem.at[m]))
    loads.append(pltpu.make_async_copy(desc_hbm, desc, lsem.at[3]))
    for p in range(Q // 2):
        columns = pl.ds(p * PAIR, PAIR)
        loads.append(pltpu.make_async_copy(cand_hbm.at[:, columns], cand.at[:, columns], lsem.at[4 + p]))
    for copy in loads:
        copy.start()

    barrier = pltpu.get_barrier_semaphore()
    partners = [at((row + d) % 16, col) for d in range(1, 16)] + [sibling]
    for i in range(8):
        partners.append(at(x * 4 + to_y, i * 2 + parity))
    for i in range(4):
        for j in range(2):
            partners.append(at(x * 4 + 2 * j + core, (2 * i + y // 2) * 2 + parity))
    for device in partners:
        pl.semaphore_signal(barrier, inc=1, device_id=device, device_id_type=MESH)

    eye = lax.broadcasted_iota(jnp.int32, (128, 128), 0) == lax.broadcasted_iota(jnp.int32, (128, 128), 1)
    on_diagonal = row == col
    factor_sends = {}
    factor_base = {}

    def encode_factor(m):
        loads[m].wait()
        block = fin[m]
        if m == 1:
            encode(fmsg.at[m], block, jnp.zeros((1, 128), F32))
        else:
            taken = eye & on_diagonal
            diagonal = jnp.sum(jnp.where(taken, block, 0.0), axis=0, keepdims=True)
            encode(fmsg.at[m], jnp.where(taken, 0.0, block), diagonal)

    def fsend_task(m):
        base = take(8)
        factor_base[m] = base
        slot = frecv.at[m, parity, z // 2, y // 2]
        for i, dz in enumerate((4, 3, 5, 2, 6, 1, 7, 0)):
            copy = pltpu.make_async_remote_copy(
                src_ref=fmsg.at[m], dst_ref=slot, send_sem=ssem.at[base + i],
                recv_sem=rsem.at[base + (z // 2) * 2 + y // 2],
                device_id=at(x * 4 + to_y, ((z + dz) % 8) * 2 + parity), device_id_type=MESH)
            if dz:
                copy.start()
                sent.append(copy)
            else:
                local = (to_y == y) & (core == parity)
                factor_sends[m] = (copy, local)

                @pl.when(jnp.logical_not(local))
                def _(copy=copy):
                    copy.start()

                @pl.when(local)
                def _():
                    frecv[m, parity, z // 2, y // 2] = fmsg[m]

    sibling_copy = {}

    def sibling_task(m):
        for i in range(4):
            for j in range(2):
                got = arrival(factor_base[m] + 2 * i + j, frecv.at[m, core, i, j])
                mine = (2 * j + core == y) & (2 * i + y // 2 == z) & (parity == core)

                @pl.when(jnp.logical_not(mine))
                def _(got=got):
                    got.wait_recv()
        sibling_copy[m] = send(frecv.at[m, core], frecv.at[m, core], sibling)

    def fac_task(m):
        arrival(sibling_copy[m], frecv.at[m, 1 - core]).wait_recv()
        for p in range(2):
            for i in range(4):
                for j in range(2):
                    value, diagonal = decode(frecv.at[m, p, i, j])
                    if m != 1:
                        value = value + jnp.where(eye, diagonal, 0.0)
                    hi, lo = split(value)
                    r = (2 * j + p) * 128
                    fbuf[m, 0, r:r + 128, i * 128:(i + 1) * 128] = hi
                    fbuf[m, 1, r:r + 128, i * 128:(i + 1) * 128] = lo

    def block_of(i):
        return pl.ds(pl.multiple_of((i % 4) * 128, 128), 128)

    gathers = {}
    scatters = {}

    def put(n, q, v):
        vown[n, q] = v
        encode(vsend.at[n, q], v)
        gathers[n, q] = [
            send(vsend.at[n, q], vrecv.at[n, q, d - 1], at(((x + 4 - d) % 4) * 4 + y, col))
            for d in (2, 1, 3)]

    def kernel_columns(panel, p):
        inner = lax.dot_general(
            desc[panel], cand[:, p * PAIR:(p + 1) * PAIR], (((0,), (0,)), ((), ())),
            preferred_element_type=F32)
        return inner * inner

    def k1_task(p):
        if p == 0:
            loads[3].wait()
        loads[4 + p].wait()
        value = kernel_columns(0, p)
        for i in range(2):
            put(0, 2 * p + i, value[:, i * CH:(i + 1) * CH])

    def k2_task(p):
        value = kernel_columns(1, p)
        for i in range(2):
            k2[2 * p + i] = value[:, i * CH:(i + 1) * CH]

    def c_task(n, q):
        hi, lo = split(vown[n, q])
        gbuf[block_of(x), 0:CH] = hi
        gbuf[block_of(x), CH:PAIR] = lo
        for k, d in zip(gathers[n, q], (2, 1, 3)):
            arrival(k, vrecv.at[n, q, d - 1]).wait_recv()
        for d in (1, 2, 3):
            value, _ = decode(vrecv.at[n, q, d - 1])
            hi, lo = split(value)
            gbuf[block_of(x + d), 0:CH] = hi
            gbuf[block_of(x + d), CH:PAIR] = lo
        v = gbuf[...]
        v_hi = v[:, 0:CH]
        for i in range(2):
            rows = slice(i * 256, (i + 1) * 256)
            both = jnp.dot(fbuf[n, 0, rows, :], v, preferred_element_type=F32)
            low = jnp.dot(fbuf[n, 1, rows, :], v_hi, preferred_element_type=F32)
            ptmp[rows, :] = both[:, 0:CH] + (both[:, CH:PAIR] + low)
        ks = []
        for d in (2, 1, 3):
            encode(psend.at[n, q, d - 1], ptmp[block_of(y + 4 - d), :])
            ks.append(send(psend.at[n, q, d - 1], precv.at[n, q, d - 1], at(x * 4 + (y + 4 - d) % 4, col)))
        scatters[n, q] = ks
        pown[n, q] = ptmp[block_of(y), :]

    def e_task(n, q):
        for k, d in zip(scatters[n, q], (2, 1, 3)):
            arrival(k, precv.at[n, q, d - 1]).wait_recv()
        value = pown[n, q]
        for d in (1, 2, 3):
            value = value + decode(precv.at[n, q, d - 1])[0]
        columns = slice(q * CH, (q + 1) * CH)
        if n == 0:
            put(1, q, value)
            first_out[:, columns] = value
            esum[q:q + 1, :] = jnp.sum(value * value, axis=0, keepdims=True)
        elif n == 1:
            put(2, q, k2[q] - value)
        else:
            esum[q:q + 1, :] = esum[q:q + 1, :] + jnp.sum(value * value, axis=0, keepdims=True)
            second_out[:, columns] = value

    esum[...] = jnp.zeros_like(esum)
    for m in range(3):
        encode_factor(m)
    pl.semaphore_wait(barrier, len(partners))
    for _, name, n, q in task_order():
        if name == "fsend":
            fsend_task(n)
        elif name == "sibling":
            sibling_task(n)
        elif name == "fac":
            fac_task(n)
        elif name == "k1":
            k1_task(q)
        elif name == "k2":
            k2_task(q)
        elif name == "c":
            c_task(n, q)
        else:
            e_task(n, q)

    ebuf[pl.ds(row, 1)] = esum[...][None]
    spread = [send(esum, ebuf.at[row], at((row + d) % 16, col)) for d in range(1, 16)]
    for d in range(1, 16):
        arrival(spread[d - 1], ebuf.at[(row + 16 - d) % 16]).wait_recv()
    total = ebuf[0]
    for i in range(1, 16):
        total = total + ebuf[i]
    ex_out[...] = total * (1.0 / (2.0 * B))

    for copy in sent:
        copy.wait_send()
    for copy, local in factor_sends.values():
        @pl.when(jnp.logical_not(local))
        def _(copy=copy):
            copy.wait_send()
    assert counter[0] <= N_SEND


def shards(inducing_desc, candidate_desc, first_inverse, coupling, second_inverse):
    hbm = pl.BlockSpec(memory_space=pl.ANY)
    vmem = pl.BlockSpec(memory_space=pltpu.VMEM)
    first, second, explained = pl.pallas_call(
        kernel,
        out_shape=(
            jax.ShapeDtypeStruct((128, Q * CH), F32),
            jax.ShapeDtypeStruct((128, Q * CH), F32),
            jax.ShapeDtypeStruct((8, 128), F32),
        ),
        in_specs=[hbm] * 5,
        out_specs=(vmem, vmem, vmem),
        scratch_shapes=[
            pltpu.VMEM((2, W, 128), BF16),
            pltpu.VMEM((W, Q * CH), BF16),
            pltpu.VMEM((3, 128, 128), F32),
            pltpu.VMEM((3, ROWS, 128), BF16),
            pltpu.VMEM((3, 2, 4, 2, ROWS, 128), BF16),
            pltpu.VMEM((3, 2, 512, 512), BF16),
            pltpu.VMEM((3, Q, 128, CH), F32),
            pltpu.VMEM((3, Q, ROWS, CH), BF16),
            pltpu.VMEM((3, Q, 3, ROWS, CH), BF16),
            pltpu.VMEM((512, PAIR), BF16),
            pltpu.VMEM((3, Q, 128, CH), F32),
            pltpu.VMEM((512, CH), F32),
            pltpu.VMEM((3, Q, 3, ROWS, CH), BF16),
            pltpu.VMEM((3, Q, 3, ROWS, CH), BF16),
            pltpu.VMEM((Q, 128, CH), F32),
            pltpu.VMEM((8, 128), F32),
            pltpu.VMEM((16, 8, 128), F32),
            pltpu.SemaphoreType.DMA((4 + Q // 2,)),
            pltpu.SemaphoreType.DMA((N_SEND,)),
            pltpu.SemaphoreType.DMA((N_SEND,)),
        ],
        compiler_params=pltpu.CompilerParams(
            collective_id=0, has_side_effects=True, vmem_limit_bytes=60 * 1024 * 1024),
    )(inducing_desc, candidate_desc, first_inverse, coupling, second_inverse)
    return first, second, explained[:Q].reshape(Q * CH)


def solution(mesh):
    return jax.shard_map(
        shards,
        mesh=mesh,
        in_specs=(
            P(None, None, "row"),
            P(None, "col"),
            P("row", "col"),
            P("row", "col"),
            P("row", "col"),
        ),
        out_specs=(P("row", "col"), P("row", "col"), P("col")),
        check_vma=False,
    )
```

```python
import jax
import jax.numpy as jnp
from jax import lax
from jax.experimental import pallas as pl
from jax.experimental.pallas import tpu as pltpu
from jax.sharding import PartitionSpec as P

W = 1960
B = 2048
CH = 128
Q = 6
PAIR = 2 * CH
MESH = pl.DeviceIdType.MESH
F32 = jnp.float32
BF16 = jnp.bfloat16

GATHER, SCATTER, FACTOR, SIBLING, SPREAD, N_RECV = 0, 18, 36, 39, 42, 43
GATHER_OUT, SCATTER_OUT, FACTOR_OUT, SIBLING_OUT, SPREAD_OUT, N_SEND = 0, 1, 2, 5, 8, 9
ROWS = 144
TINY = 1e-35


def split(v):
    hi = v.astype(BF16)
    lo = (v - hi.astype(F32)).astype(BF16)
    return hi, lo


def encode(ref, v, diagonal=None):
    top = jnp.max(jnp.abs(v), axis=0, keepdims=True)
    s = (top * 1.01 + TINY).astype(BF16)
    t = jnp.abs(v) * (250.0 / s.astype(F32))
    e = jnp.floor(t)
    c = jnp.exp2(e - 125.0) * ((t - e) + 1.0)
    ref[0:128, :] = jnp.where(v < 0.0, -c, c).astype(BF16)
    tail = jnp.broadcast_to(s.astype(F32), (16, 128))
    if diagonal is not None:
        hi, lo = split(diagonal)
        index = lax.broadcasted_iota(jnp.int32, (16, 128), 0)
        tail = jnp.where(index == 1, hi.astype(F32), jnp.where(index == 2, lo.astype(F32), tail))
    ref[128:144, :] = tail.astype(BF16)


def decode(ref):
    c = ref[0:128, :].astype(F32)
    tail = ref[128:144, :].astype(F32)
    a = jnp.abs(c)
    e = jnp.floor(jnp.log2(a) + 0.002)
    t = (e + (a * jnp.exp2(-e) + 124.0)) * (tail[0:1, :] * (1.0 / 250.0))
    return jnp.where(c < 0.0, -t, t), tail[1:2, :] + tail[2:3, :]


def task_order():
    tasks = []
    start, period, step, flight = 14.0, 10.6, 1.65, 5.2
    for n in range(3):
        for q in range(Q):
            t = start + n * period + q * step
            tasks.append((t, "c", n, q))
            tasks.append((t + flight, "e", n, q))
    for p in range(Q // 2):
        tasks.append((3.0 + 0.5 * p, "k1", 0, p))
        tasks.append((5.0 + 0.5 * p, "k2", 0, p))
    for m in range(3):
        tasks.append(((2.0, 7.0, 13.0)[m], "fsend", m, 0))
        tasks.append(((10.0, 16.0, 24.0)[m], "sibling", m, 0))
        tasks.append(((13.9, 20.0, 30.0)[m], "fac", m, 0))
    tasks.sort()
    return tasks


def kernel(desc_hbm, cand_hbm, f_hbm, c_hbm, s_hbm, first_out, second_out, ex_out,
           desc, cand, fin, fmsg, frecv, fbuf, vown, vsend, vrecv, gbuf, pown, ptmp, psend, precv,
           k2, esum, ebuf, lsem, ssem, rsem):
    row = lax.axis_index("row")
    col = lax.axis_index("col")
    x, y = row // 4, row % 4
    z, core = col // 2, col % 2

    def at(r, c):
        return {"row": r, "col": c}

    sibling = at(row, z * 2 + 1 - core)
    to_y = 2 * (z % 2) + core
    parity = y % 2

    def remote(src, dst, out, into, device):
        return pltpu.make_async_remote_copy(
            src_ref=src, dst_ref=dst, send_sem=ssem.at[out], recv_sem=rsem.at[into],
            device_id=device, device_id_type=MESH)

    def arrived(into, ref):
        remote(ref, ref, 0, into, sibling).wait_recv()

    def departed(out, ref):
        remote(ref, ref, out, 0, sibling).wait_send()

    loads = []
    for m, ref in enumerate((f_hbm, c_hbm, s_hbm)):
        loads.append(pltpu.make_async_copy(ref, fin.at[m], lsem.at[m]))
    loads.append(pltpu.make_async_copy(desc_hbm, desc, lsem.at[3]))
    for p in range(Q // 2):
        columns = pl.ds(p * PAIR, PAIR)
        loads.append(pltpu.make_async_copy(cand_hbm.at[:, columns], cand.at[:, columns], lsem.at[4 + p]))
    for copy in loads:
        copy.start()

    barrier = pltpu.get_barrier_semaphore()
    partners = [at((row + d) % 16, col) for d in range(1, 16)] + [sibling]
    for i in range(4):
        for j in range(2):
            partners.append(at(x * 4 + 2 * j + core, (2 * i + y // 2) * 2 + parity))
    for device in partners:
        pl.semaphore_signal(barrier, inc=1, device_id=device, device_id_type=MESH)

    eye = lax.broadcasted_iota(jnp.int32, (128, 128), 0) == lax.broadcasted_iota(jnp.int32, (128, 128), 1)
    on_diagonal = row == col
    def encode_factor(m):
        loads[m].wait()
        block = fin[m]
        if m == 1:
            encode(fmsg.at[m], block, jnp.zeros((1, 128), F32))
        else:
            taken = eye & on_diagonal
            diagonal = jnp.sum(jnp.where(taken, block, 0.0), axis=0, keepdims=True)
            encode(fmsg.at[m], jnp.where(taken, 0.0, block), diagonal)

    here = (to_y == y) & (core == parity)
    my_slot = pl.ds(pl.multiple_of(((z // 2) * 2 + y // 2) * ROWS, 16), ROWS)

    def fsend_task(m):
        slot = frecv.at[m, parity, my_slot]
        for dz in (4, 3, 5, 2, 6, 1, 7, 0):
            copy = remote(fmsg.at[m], slot, FACTOR_OUT + m, FACTOR + m,
                          at(x * 4 + to_y, ((z + dz) % 8) * 2 + parity))
            if dz:
                copy.start()
            else:
                @pl.when(jnp.logical_not(here))
                def _():
                    copy.start()

                @pl.when(here)
                def _():
                    pltpu.make_async_copy(fmsg.at[m], slot, rsem.at[FACTOR + m]).start()

    def sibling_task(m):
        arrived(FACTOR + m, frecv.at[m, core])
        remote(frecv.at[m, core], frecv.at[m, core], SIBLING_OUT + m, SIBLING + m, sibling).start()

    def fac_task(m):
        arrived(SIBLING + m, frecv.at[m, 1 - core])
        for p in range(2):
            for i in range(4):
                for j in range(2):
                    value, diagonal = decode(frecv.at[m, p, pl.ds((2 * i + j) * ROWS, ROWS)])
                    if m != 1:
                        value = value + jnp.where(eye, diagonal, 0.0)
                    hi, lo = split(value)
                    r = (2 * j + p) * 128
                    fbuf[m, 0, r:r + 128, i * 128:(i + 1) * 128] = hi
                    fbuf[m, 1, r:r + 128, i * 128:(i + 1) * 128] = lo

    def block_of(i):
        return pl.ds(pl.multiple_of((i % 4) * 128, 128), 128)

    def put(n, q, v):
        vown[n, q] = v
        encode(vsend.at[n, q], v)
        for d in (2, 1, 3):
            remote(vsend.at[n, q], vrecv.at[n, q, d - 1], GATHER_OUT, GATHER + n * Q + q,
                   at(((x + 4 - d) % 4) * 4 + y, col)).start()

    def kernel_columns(panel, p):
        inner = lax.dot_general(
            desc[panel], cand[:, p * PAIR:(p + 1) * PAIR], (((0,), (0,)), ((), ())),
            preferred_element_type=F32)
        return inner * inner

    def k1_task(p):
        if p == 0:
            loads[3].wait()
        loads[4 + p].wait()
        value = kernel_columns(0, p)
        for i in range(2):
            put(0, 2 * p + i, value[:, i * CH:(i + 1) * CH])

    def k2_task(p):
        value = kernel_columns(1, p)
        for i in range(2):
            k2[2 * p + i] = value[:, i * CH:(i + 1) * CH]

    def c_task(n, q):
        hi, lo = split(vown[n, q])
        gbuf[block_of(x), 0:CH] = hi
        gbuf[block_of(x), CH:PAIR] = lo
        arrived(GATHER + n * Q + q, vrecv.at[n, q])
        for d in (1, 2, 3):
            value, _ = decode(vrecv.at[n, q, d - 1])
            hi, lo = split(value)
            gbuf[block_of(x + d), 0:CH] = hi
            gbuf[block_of(x + d), CH:PAIR] = lo
        v = gbuf[...]
        v_hi = v[:, 0:CH]
        for i in range(2):
            rows = slice(i * 256, (i + 1) * 256)
            both = jnp.dot(fbuf[n, 0, rows, :], v, preferred_element_type=F32)
            low = jnp.dot(fbuf[n, 1, rows, :], v_hi, preferred_element_type=F32)
            ptmp[rows, :] = both[:, 0:CH] + (both[:, CH:PAIR] + low)
        for d in (2, 1, 3):
            encode(psend.at[n, q, d - 1], ptmp[block_of(y + 4 - d), :])
            remote(psend.at[n, q, d - 1], precv.at[n, q, d - 1], SCATTER_OUT, SCATTER + n * Q + q,
                   at(x * 4 + (y + 4 - d) % 4, col)).start()
        pown[n, q] = ptmp[block_of(y), :]

    def e_task(n, q):
        arrived(SCATTER + n * Q + q, precv.at[n, q])
        value = pown[n, q]
        for d in (1, 2, 3):
            value = value + decode(precv.at[n, q, d - 1])[0]
        columns = slice(q * CH, (q + 1) * CH)
        if n == 0:
            put(1, q, value)
            first_out[:, columns] = value
            esum[q:q + 1, :] = jnp.sum(value * value, axis=0, keepdims=True)
        elif n == 1:
            put(2, q, k2[q] - value)
        else:
            esum[q:q + 1, :] = esum[q:q + 1, :] + jnp.sum(value * value, axis=0, keepdims=True)
            second_out[:, columns] = value

    esum[...] = jnp.zeros_like(esum)
    for m in range(3):
        encode_factor(m)
    pl.semaphore_wait(barrier, len(partners))
    for _, name, n, q in task_order():
        if name == "fsend":
            fsend_task(n)
        elif name == "sibling":
            sibling_task(n)
        elif name == "fac":
            fac_task(n)
        elif name == "k1":
            k1_task(q)
        elif name == "k2":
            k2_task(q)
        elif name == "c":
            c_task(n, q)
        else:
            e_task(n, q)

    ebuf[pl.ds(row, 1)] = esum[...][None]
    for d in range(1, 16):
        remote(esum, ebuf.at[row], SPREAD_OUT, SPREAD, at((row + d) % 16, col)).start()
    arrived(SPREAD, ebuf.at[pl.ds(0, 15)])
    total = ebuf[0]
    for i in range(1, 16):
        total = total + ebuf[i]
    ex_out[...] = total * (1.0 / (2.0 * B))

    departed(GATHER_OUT, vrecv)
    departed(SCATTER_OUT, precv)
    departed(SPREAD_OUT, ebuf.at[pl.ds(0, 15)])
    for m in range(3):
        departed(SIBLING_OUT + m, frecv.at[m, core])

        @pl.when(here)
        def _():
            departed(FACTOR_OUT + m, frecv.at[m, 0, pl.ds(0, 7 * ROWS)])

        @pl.when(jnp.logical_not(here))
        def _():
            departed(FACTOR_OUT + m, frecv.at[m, 0])


def finish(first, second, explained, first_out, second_out, explained_out):
    first_out[...] = first[...]
    second_out[...] = second[...]
    for q in range(Q):
        explained_out[q * CH:(q + 1) * CH] = explained[q, :]


def shards(inducing_desc, candidate_desc, first_inverse, coupling, second_inverse):
    hbm = pl.BlockSpec(memory_space=pl.ANY)
    vmem = pl.BlockSpec(memory_space=pltpu.VMEM)
    first, second, explained = pl.pallas_call(
        kernel,
        out_shape=(
            jax.ShapeDtypeStruct((128, Q * CH), F32),
            jax.ShapeDtypeStruct((128, Q * CH), F32),
            jax.ShapeDtypeStruct((8, 128), F32),
        ),
        in_specs=[hbm] * 5,
        out_specs=(vmem, vmem, vmem),
        scratch_shapes=[
            pltpu.VMEM((2, W, 128), BF16),
            pltpu.VMEM((W, Q * CH), BF16),
            pltpu.VMEM((3, 128, 128), F32),
            pltpu.VMEM((3, ROWS, 128), BF16),
            pltpu.VMEM((3, 2, 8 * ROWS, 128), BF16),
            pltpu.VMEM((3, 2, 512, 512), BF16),
            pltpu.VMEM((3, Q, 128, CH), F32),
            pltpu.VMEM((3, Q, ROWS, CH), BF16),
            pltpu.VMEM((3, Q, 3, ROWS, CH), BF16),
            pltpu.VMEM((512, PAIR), BF16),
            pltpu.VMEM((3, Q, 128, CH), F32),
            pltpu.VMEM((512, CH), F32),
            pltpu.VMEM((3, Q, 3, ROWS, CH), BF16),
            pltpu.VMEM((3, Q, 3, ROWS, CH), BF16),
            pltpu.VMEM((Q, 128, CH), F32),
            pltpu.VMEM((8, 128), F32),
            pltpu.VMEM((16, 8, 128), F32),
            pltpu.SemaphoreType.DMA((4 + Q // 2,)),
            pltpu.SemaphoreType.DMA((N_SEND,)),
            pltpu.SemaphoreType.DMA((N_RECV,)),
        ],
        compiler_params=pltpu.CompilerParams(
            collective_id=0, has_side_effects=True, vmem_limit_bytes=60 * 1024 * 1024),
    )(inducing_desc, candidate_desc, first_inverse, coupling, second_inverse)
    return pl.pallas_call(
        finish,
        out_shape=(
            jax.ShapeDtypeStruct((128, Q * CH), F32),
            jax.ShapeDtypeStruct((128, Q * CH), F32),
            jax.ShapeDtypeStruct((Q * CH,), F32),
        ),
        in_specs=[vmem] * 3,
        out_specs=(vmem, vmem, vmem),
    )(first, second, explained)


def solution(mesh):
    return jax.shard_map(
        shards,
        mesh=mesh,
        in_specs=(
            P(None, None, "row"),
            P(None, "col"),
            P("row", "col"),
            P("row", "col"),
            P("row", "col"),
        ),
        out_specs=(P("row", "col"), P("row", "col"), P("col")),
        check_vma=False,
    )
```

```python
import jax
import jax.numpy as jnp
from jax import lax
from jax.experimental import pallas as pl
from jax.experimental.pallas import tpu as pltpu
from jax.sharding import PartitionSpec as P

W = 1960
B = 2048
CH = 128
Q = 6
PAIR = 2 * CH
MESH = pl.DeviceIdType.MESH
F32 = jnp.float32
BF16 = jnp.bfloat16

GATHER, SCATTER, FACTOR, SIBLING, SPREAD, GATHER_C, SCATTER_T, N_RECV = 0, 18, 30, 33, 36, 37, 38, 39
GATHER_OUT, SCATTER_OUT, FACTOR_OUT, SIBLING_OUT, SPREAD_OUT, C_OUT, T_OUT, N_SEND = 0, 1, 2, 5, 8, 9, 10, 11
ROWS = 144
TINY = 1e-35


def split(v):
    hi = v.astype(BF16)
    lo = (v - hi.astype(F32)).astype(BF16)
    return hi, lo


def encode(ref, v, diagonal=None):
    top = jnp.max(jnp.abs(v), axis=0, keepdims=True)
    s = (top * 1.01 + TINY).astype(BF16)
    t = jnp.abs(v) * (250.0 / s.astype(F32))
    e = jnp.floor(t)
    c = jnp.exp2(e - 125.0) * ((t - e) + 1.0)
    ref[0:128, :] = jnp.where(v < 0.0, -c, c).astype(BF16)
    tail = jnp.broadcast_to(s.astype(F32), (16, 128))
    if diagonal is not None:
        hi, lo = split(diagonal)
        index = lax.broadcasted_iota(jnp.int32, (16, 128), 0)
        tail = jnp.where(index == 1, hi.astype(F32), jnp.where(index == 2, lo.astype(F32), tail))
    ref[128:144, :] = tail.astype(BF16)


def decode(ref):
    c = ref[0:128, :].astype(F32)
    tail = ref[128:144, :].astype(F32)
    a = jnp.abs(c)
    e = jnp.floor(jnp.log2(a) + 0.002)
    t = (e + (a * jnp.exp2(-e) + 124.0)) * (tail[0:1, :] * (1.0 / 250.0))
    return jnp.where(c < 0.0, -t, t), tail[1:2, :] + tail[2:3, :]


TASKS = (
    ("fsend", 2, 0), ("fsend", 0, 0), ("coupling", 0, 0), ("k", 0, 0), ("k", 0, 1), ("k", 0, 2), ("k", 1, 0),
    ("k", 1, 1), ("k", 1, 2), ("sibling", 2, 0), ("fac", 2, 0), ("ct", 0, 0), ("sibling", 0, 0), ("et", 0, 0),
    ("fac", 0, 0), ("c", 0, 0), ("c", 0, 1), ("c", 0, 2), ("c", 0, 3), ("c", 0, 4), ("c", 0, 5), ("e", 0, 0),
    ("e", 0, 1), ("e", 0, 2), ("sibling", 1, 0), ("e", 0, 3), ("fac", 1, 0), ("c", 1, 0), ("e", 0, 4),
    ("c", 1, 1), ("e", 0, 5), ("c", 1, 2), ("c", 1, 3), ("e", 1, 0), ("c", 1, 4), ("e", 1, 1), ("c", 1, 5),
    ("e", 1, 2), ("e", 1, 3), ("e", 1, 4), ("e", 1, 5),
)


def kernel(desc_hbm, cand_hbm, f_hbm, c_hbm, s_hbm, first_out, second_out, ex_out,
           desc, cand, fin, fmsg, frecv, fbuf, vown, vsend, vrecv, gbuf, pown, ptmp, psend, precv,
           csend, crecv, tsend, trecv, town, esum, ebuf, lsem, ssem, rsem):
    row = lax.axis_index("row")
    col = lax.axis_index("col")
    x, y = row // 4, row % 4
    z, core = col // 2, col % 2

    def at(r, c):
        return {"row": r, "col": c}

    sibling = at(row, z * 2 + 1 - core)
    to_y = 2 * (z % 2) + core
    parity = y % 2

    def remote(src, dst, out, into, device):
        return pltpu.make_async_remote_copy(
            src_ref=src, dst_ref=dst, send_sem=ssem.at[out], recv_sem=rsem.at[into],
            device_id=device, device_id_type=MESH)

    def arrived(into, ref):
        remote(ref, ref, 0, into, sibling).wait_recv()

    def departed(out, ref):
        remote(ref, ref, out, 0, sibling).wait_send()

    barrier = pltpu.get_barrier_semaphore()
    partners = [at((row + d) % 16, col) for d in range(1, 16)] + [sibling]
    for i in range(4):
        for j in range(2):
            partners.append(at(x * 4 + 2 * j + core, (2 * i + y // 2) * 2 + parity))
    for device in partners:
        pl.semaphore_signal(barrier, inc=1, device_id=device, device_id_type=MESH)

    loads = []
    for m, ref in enumerate((f_hbm, c_hbm, s_hbm)):
        loads.append(pltpu.make_async_copy(ref, fin.at[m], lsem.at[m]))
    loads.append(pltpu.make_async_copy(desc_hbm, desc, lsem.at[3]))
    for p in range(Q // 2):
        columns = pl.ds(p * PAIR, PAIR)
        loads.append(pltpu.make_async_copy(cand_hbm.at[:, columns], cand.at[:, columns], lsem.at[4 + p]))
    for copy in loads:
        copy.start()

    eye = lax.broadcasted_iota(jnp.int32, (128, 128), 0) == lax.broadcasted_iota(jnp.int32, (128, 128), 1)
    on_diagonal = row == col
    def encode_factor(m):
        loads[m].wait()
        block = fin[m]
        taken = eye & on_diagonal
        diagonal = jnp.sum(jnp.where(taken, block, 0.0), axis=0, keepdims=True)
        encode(fmsg.at[m], jnp.where(taken, 0.0, block), diagonal)

    here = (to_y == y) & (core == parity)
    my_slot = pl.ds(pl.multiple_of(((z // 2) * 2 + y // 2) * ROWS, 16), ROWS)

    def fsend_task(m):
        slot = frecv.at[m, parity, my_slot]
        for dz in (4, 3, 5, 2, 6, 1, 7, 0):
            copy = remote(fmsg.at[m], slot, FACTOR_OUT + m, FACTOR + m,
                          at(x * 4 + to_y, ((z + dz) % 8) * 2 + parity))
            if dz:
                copy.start()
            else:
                @pl.when(jnp.logical_not(here))
                def _():
                    copy.start()

                @pl.when(here)
                def _():
                    pltpu.make_async_copy(fmsg.at[m], slot, rsem.at[FACTOR + m]).start()

    def sibling_task(m):
        arrived(FACTOR + m, frecv.at[m, core])
        remote(frecv.at[m, core], frecv.at[m, core], SIBLING_OUT + m, SIBLING + m, sibling).start()

    def fac_task(m):
        arrived(SIBLING + m, frecv.at[m, 1 - core])
        for p in range(2):
            for i in range(4):
                for j in range(2):
                    value, diagonal = decode(frecv.at[m, p, pl.ds((2 * i + j) * ROWS, ROWS)])
                    if m != 1:
                        value = value + jnp.where(eye, diagonal, 0.0)
                    hi, lo = split(value)
                    r = (2 * j + p) * 128
                    fbuf[m, 0, r:r + 128, i * 128:(i + 1) * 128] = hi
                    fbuf[m, 1, r:r + 128, i * 128:(i + 1) * 128] = lo

    def block_of(i):
        return pl.ds(pl.multiple_of((i % 4) * 128, 128), 128)

    def spread_over(send_ref, recv_ref, out, into, d, device):
        remote(send_ref, recv_ref.at[d - 1], out, into, device).start()

    def over_x(d):
        return at(((x + 4 - d) % 4) * 4 + y, col)

    def over_y(d):
        return at(x * 4 + (y + 4 - d) % 4, col)

    def put(n, q, v):
        vown[n, q] = v
        encode(vsend.at[n, q], v)
        for d in (2, 1, 3):
            spread_over(vsend.at[n, q], vrecv.at[n, q], GATHER_OUT, GATHER + n * Q + q, d, over_x(d))

    def coupling_task():
        loads[1].wait()
        encode(csend, fin[1])
        for d in (2, 1, 3):
            spread_over(csend, crecv, C_OUT, GATHER_C, d, over_x(d))

    def kernel_columns(panel, p):
        inner = lax.dot_general(
            desc[panel], cand[:, p * PAIR:(p + 1) * PAIR], (((0,), (0,)), ((), ())),
            preferred_element_type=F32)
        return inner * inner

    def k_task(panel, p):
        if panel == 0:
            if p == 0:
                loads[3].wait()
            loads[4 + p].wait()
        value = kernel_columns(panel, p)
        for i in range(2):
            put(panel, 2 * p + i, value[:, i * CH:(i + 1) * CH])

    def fill(g, own, recv):
        hi, lo = split(own)
        gbuf[g, block_of(x), 0:CH] = hi
        gbuf[g, block_of(x), CH:PAIR] = lo
        for d in (1, 2, 3):
            hi, lo = split(decode(recv.at[d - 1])[0])
            gbuf[g, block_of(x + d), 0:CH] = hi
            gbuf[g, block_of(x + d), CH:PAIR] = lo

    def product(m, g, rows):
        both = jnp.dot(fbuf[m, 0, rows, :], gbuf[g], preferred_element_type=F32)
        low = jnp.dot(fbuf[m, 1, rows, :], gbuf[g, :, 0:CH], preferred_element_type=F32)
        return both[:, 0:CH] + (both[:, CH:PAIR] + low)

    def scatter(send_ref, recv_ref, out, into):
        for d in (2, 1, 3):
            encode(send_ref.at[d - 1], ptmp[block_of(y + 4 - d), :])
            spread_over(send_ref.at[d - 1], recv_ref, out, into, d, over_y(d))

    def collect(own, recv):
        value = own
        for d in (1, 2, 3):
            value = value + decode(recv.at[d - 1])[0]
        return value

    halves = (slice(0, 256), slice(256, 512))

    def ct_task():
        arrived(GATHER_C, crecv)
        fill(0, fin[1], crecv)
        for rows in halves:
            ptmp[rows, :] = product(2, 0, rows)
        scatter(tsend, trecv, T_OUT, SCATTER_T)
        town[...] = ptmp[block_of(y), :]

    def et_task():
        arrived(SCATTER_T, trecv)
        encode(fmsg.at[1], collect(town[...], trecv), jnp.zeros((1, 128), F32))
        fsend_task(1)

    def c_task(n, q):
        arrived(GATHER + n * Q + q, vrecv.at[n, q])
        fill(0, vown[n, q], vrecv.at[n, q])
        if n == 0:
            for rows in halves:
                ptmp[rows, :] = product(0, 0, rows)
        else:
            arrived(GATHER + 2 * Q + q, vrecv.at[2, q])
            fill(1, vown[2, q], vrecv.at[2, q])
            for rows in halves:
                ptmp[rows, :] = product(2, 0, rows) - product(1, 1, rows)
        scatter(psend.at[n, q], precv.at[n, q], SCATTER_OUT, SCATTER + n * Q + q)
        pown[n, q] = ptmp[block_of(y), :]

    def e_task(n, q):
        arrived(SCATTER + n * Q + q, precv.at[n, q])
        value = collect(pown[n, q], precv.at[n, q])
        columns = slice(q * CH, (q + 1) * CH)
        if n == 0:
            put(2, q, value)
            first_out[:, columns] = value
            esum[q:q + 1, :] = jnp.sum(value * value, axis=0, keepdims=True)
        else:
            esum[q:q + 1, :] = esum[q:q + 1, :] + jnp.sum(value * value, axis=0, keepdims=True)
            second_out[:, columns] = value

    esum[...] = jnp.zeros_like(esum)
    encode_factor(2)
    encode_factor(0)
    pl.semaphore_wait(barrier, len(partners))
    run = {
        "fsend": lambda n, q: fsend_task(n), "sibling": lambda n, q: sibling_task(n),
        "fac": lambda n, q: fac_task(n), "coupling": lambda n, q: coupling_task(),
        "k": k_task, "ct": lambda n, q: ct_task(), "et": lambda n, q: et_task(),
        "c": c_task, "e": e_task,
    }
    for name, n, q in TASKS:
        run[name](n, q)

    ebuf[pl.ds(row, 1)] = esum[...][None]
    for d in range(1, 16):
        remote(esum, ebuf.at[row], SPREAD_OUT, SPREAD, at((row + d) % 16, col)).start()
    arrived(SPREAD, ebuf.at[pl.ds(0, 15)])
    total = ebuf[0]
    for i in range(1, 16):
        total = total + ebuf[i]
    ex_out[...] = total * (1.0 / (2.0 * B))

    departed(GATHER_OUT, vrecv)
    departed(SCATTER_OUT, precv)
    departed(C_OUT, crecv)
    departed(T_OUT, trecv)
    departed(SPREAD_OUT, ebuf.at[pl.ds(0, 15)])
    for m in range(3):
        departed(SIBLING_OUT + m, frecv.at[m, core])

        @pl.when(here)
        def _():
            departed(FACTOR_OUT + m, frecv.at[m, 0, pl.ds(0, 7 * ROWS)])

        @pl.when(jnp.logical_not(here))
        def _():
            departed(FACTOR_OUT + m, frecv.at[m, 0])


def finish(first, second, explained, first_out, second_out, explained_out):
    first_out[...] = first[...]
    second_out[...] = second[...]
    for q in range(Q):
        explained_out[q * CH:(q + 1) * CH] = explained[q, :]


def shards(inducing_desc, candidate_desc, first_inverse, coupling, second_inverse):
    hbm = pl.BlockSpec(memory_space=pl.ANY)
    vmem = pl.BlockSpec(memory_space=pltpu.VMEM)
    first, second, explained = pl.pallas_call(
        kernel,
        out_shape=(
            jax.ShapeDtypeStruct((128, Q * CH), F32),
            jax.ShapeDtypeStruct((128, Q * CH), F32),
            jax.ShapeDtypeStruct((8, 128), F32),
        ),
        in_specs=[hbm] * 5,
        out_specs=(vmem, vmem, vmem),
        scratch_shapes=[
            pltpu.VMEM((2, W, 128), BF16),
            pltpu.VMEM((W, Q * CH), BF16),
            pltpu.VMEM((3, 128, 128), F32),
            pltpu.VMEM((3, ROWS, 128), BF16),
            pltpu.VMEM((3, 2, 8 * ROWS, 128), BF16),
            pltpu.VMEM((3, 2, 512, 512), BF16),
            pltpu.VMEM((3, Q, 128, CH), F32),
            pltpu.VMEM((3, Q, ROWS, CH), BF16),
            pltpu.VMEM((3, Q, 3, ROWS, CH), BF16),
            pltpu.VMEM((2, 512, PAIR), BF16),
            pltpu.VMEM((2, Q, 128, CH), F32),
            pltpu.VMEM((512, CH), F32),
            pltpu.VMEM((2, Q, 3, ROWS, CH), BF16),
            pltpu.VMEM((2, Q, 3, ROWS, CH), BF16),
            pltpu.VMEM((ROWS, 128), BF16),
            pltpu.VMEM((3, ROWS, 128), BF16),
            pltpu.VMEM((3, ROWS, 128), BF16),
            pltpu.VMEM((3, ROWS, 128), BF16),
            pltpu.VMEM((128, 128), F32),
            pltpu.VMEM((8, 128), F32),
            pltpu.VMEM((16, 8, 128), F32),
            pltpu.SemaphoreType.DMA((4 + Q // 2,)),
            pltpu.SemaphoreType.DMA((N_SEND,)),
            pltpu.SemaphoreType.DMA((N_RECV,)),
        ],
        compiler_params=pltpu.CompilerParams(
            collective_id=0, has_side_effects=True, vmem_limit_bytes=60 * 1024 * 1024),
    )(inducing_desc, candidate_desc, first_inverse, coupling, second_inverse)
    return pl.pallas_call(
        finish,
        out_shape=(
            jax.ShapeDtypeStruct((128, Q * CH), F32),
            jax.ShapeDtypeStruct((128, Q * CH), F32),
            jax.ShapeDtypeStruct((Q * CH,), F32),
        ),
        in_specs=[vmem] * 3,
        out_specs=(vmem, vmem, vmem),
    )(first, second, explained)


def solution(mesh):
    return jax.shard_map(
        shards,
        mesh=mesh,
        in_specs=(
            P(None, None, "row"),
            P(None, "col"),
            P("row", "col"),
            P("row", "col"),
            P("row", "col"),
        ),
        out_specs=(P("row", "col"), P("row", "col"), P("col")),
        check_vma=False,
    )
```

```python
import jax
import jax.numpy as jnp
from jax import lax
from jax.experimental import pallas as pl
from jax.experimental.pallas import tpu as pltpu
from jax.sharding import PartitionSpec as P

W = 1960
B = 2048
CH = 128
Q = 6
PAIR = 2 * CH
MESH = pl.DeviceIdType.MESH
F32 = jnp.float32
BF16 = jnp.bfloat16

GATHER, SCATTER, FACTOR, SIBLING, SPREAD, GATHER_C, SCATTER_T, N_RECV = 0, 18, 30, 42, 45, 46, 47, 48
GATHER_OUT, SCATTER_OUT, FACTOR_OUT, SIBLING_OUT, SPREAD_OUT, C_OUT, T_OUT, N_SEND = 0, 1, 2, 5, 8, 9, 10, 11
ROWS = 144
TINY = 1e-35


def split(v):
    hi = v.astype(BF16)
    lo = (v - hi.astype(F32)).astype(BF16)
    return hi, lo


def encode(ref, v, diagonal=None):
    top = jnp.max(jnp.abs(v), axis=0, keepdims=True)
    s = (top * 1.01 + TINY).astype(BF16)
    t = jnp.abs(v) * (250.0 / s.astype(F32))
    e = jnp.floor(t)
    c = jnp.exp2(e - 125.0) * ((t - e) + 1.0)
    ref[0:128, :] = jnp.where(v < 0.0, -c, c).astype(BF16)
    tail = jnp.broadcast_to(s.astype(F32), (16, 128))
    if diagonal is not None:
        hi, lo = split(diagonal)
        index = lax.broadcasted_iota(jnp.int32, (16, 128), 0)
        tail = jnp.where(index == 1, hi.astype(F32), jnp.where(index == 2, lo.astype(F32), tail))
    ref[128:144, :] = tail.astype(BF16)


def decode(ref):
    c = ref[0:128, :].astype(F32)
    tail = ref[128:144, :].astype(F32)
    a = jnp.abs(c)
    e = jnp.floor(jnp.log2(a) + 0.002)
    t = (e + (a * jnp.exp2(-e) + 124.0)) * (tail[0:1, :] * (1.0 / 250.0))
    return jnp.where(c < 0.0, -t, t), tail[1:2, :] + tail[2:3, :]


TASKS = (
    ("fsend", 2, 0), ("fsend", 0, 0), ("coupling", 0, 0), ("k", 0, 0), ("k", 0, 1), ("k", 0, 2), ("k", 1, 0),
    ("k", 1, 1), ("k", 1, 2), ("sibling", 2, 0), ("fac", 2, 0), ("ct", 0, 0), ("sibling", 0, 0), ("et", 0, 0),
    ("fac", 0, 0), ("c", 0, 0), ("c", 0, 1), ("c", 0, 2), ("c", 0, 3), ("c", 0, 4), ("c", 0, 5), ("s", 0, 0),
    ("s", 0, 1), ("s", 0, 2), ("s", 0, 3), ("e", 0, 0), ("s", 0, 4), ("e", 0, 1), ("s", 0, 5), ("e", 0, 2),
    ("sibling", 1, 0), ("e", 0, 3), ("fac", 1, 0), ("c", 1, 0), ("e", 0, 4), ("c", 1, 1), ("e", 0, 5),
    ("c", 1, 2), ("c", 1, 3), ("e", 1, 0), ("c", 1, 4), ("e", 1, 1), ("c", 1, 5), ("e", 1, 2), ("e", 1, 3),
    ("e", 1, 4), ("e", 1, 5),
)


def kernel(desc_hbm, cand_hbm, f_hbm, c_hbm, s_hbm, first_out, second_out, ex_out,
           desc, cand, fin, fmsg, frecv, fbuf, vown, vsend, vrecv, gbuf, pown, ptmp, psend, precv,
           csend, crecv, tsend, trecv, town, sk2, second, esum, ebuf, lsem, ssem, rsem):
    row = lax.axis_index("row")
    col = lax.axis_index("col")
    x, y = row // 4, row % 4
    z, core = col // 2, col % 2

    def at(r, c):
        return {"row": r, "col": c}

    sibling = at(row, z * 2 + 1 - core)
    to_y = 2 * (z % 2) + core
    parity = y % 2

    def remote(src, dst, out, into, device):
        return pltpu.make_async_remote_copy(
            src_ref=src, dst_ref=dst, send_sem=ssem.at[out], recv_sem=rsem.at[into],
            device_id=device, device_id_type=MESH)

    def arrived(into, ref):
        remote(ref, ref, 0, into, sibling).wait_recv()

    def departed(out, ref):
        remote(ref, ref, out, 0, sibling).wait_send()

    barrier = pltpu.get_barrier_semaphore()
    partners = []
    for i in range(4):
        for j in range(2):
            partners.append(at(x * 4 + 2 * j + core, (2 * ((z // 2 + i + 1) % 4) + y // 2) * 2 + parity))
    partners += [at((row + d) % 16, col) for d in range(1, 16)] + [sibling]
    for device in partners:
        pl.semaphore_signal(barrier, inc=1, device_id=device, device_id_type=MESH)

    loads = []
    for m, ref in enumerate((f_hbm, c_hbm, s_hbm)):
        loads.append(pltpu.make_async_copy(ref, fin.at[m], lsem.at[m]))
    loads.append(pltpu.make_async_copy(desc_hbm, desc, lsem.at[3]))
    for p in range(Q // 2):
        columns = pl.ds(p * PAIR, PAIR)
        loads.append(pltpu.make_async_copy(cand_hbm.at[:, columns], cand.at[:, columns], lsem.at[4 + p]))
    for copy in loads:
        copy.start()

    eye = lax.broadcasted_iota(jnp.int32, (128, 128), 0) == lax.broadcasted_iota(jnp.int32, (128, 128), 1)
    on_diagonal = row == col
    def encode_factor(m):
        loads[m].wait()
        block = fin[m]
        taken = eye & on_diagonal
        diagonal = jnp.sum(jnp.where(taken, block, 0.0), axis=0, keepdims=True)
        encode(fmsg.at[m], jnp.where(taken, 0.0, block), diagonal)

    here = (to_y == y) & (core == parity)
    my_slot = pl.ds(pl.multiple_of(((z // 2) * 2 + y // 2) * ROWS, 16), ROWS)

    def fsend_task(m):
        slot = frecv.at[m, parity, my_slot]
        for dz in (4, 3, 5, 2, 6, 1, 7, 0):
            to_z = (z + dz) % 8
            into = FACTOR + 4 * m + (z // 2 + 4 - to_z // 2) % 4
            copy = remote(fmsg.at[m], slot, FACTOR_OUT + m, into, at(x * 4 + to_y, to_z * 2 + parity))
            if dz:
                copy.start()
            else:
                @pl.when(jnp.logical_not(here))
                def _():
                    copy.start()

                @pl.when(here)
                def _():
                    pltpu.make_async_copy(fmsg.at[m], slot, rsem.at[FACTOR + 4 * m]).start()

    def sibling_task(m):
        for k in (2, 1, 3, 0):
            strip = (z // 2 + k) % 4
            got = frecv.at[m, core, pl.ds(pl.multiple_of(strip * (2 * ROWS), 2 * ROWS), 2 * ROWS)]
            arrived(FACTOR + 4 * m + k, got)
            remote(got, got, SIBLING_OUT + m, SIBLING + m, sibling).start()
        decode_factor(m, core)

    def decode_factor(m, p):
        for i in range(4):
            for j in range(2):
                value, diagonal = decode(frecv.at[m, p, pl.ds((2 * i + j) * ROWS, ROWS)])
                if m != 1:
                    value = value + jnp.where(eye, diagonal, 0.0)
                hi, lo = split(value)
                rows = pl.ds(pl.multiple_of(2 * j * 128 + p * 128, 128), 128)
                fbuf[m, 0, rows, i * 128:(i + 1) * 128] = hi
                fbuf[m, 1, rows, i * 128:(i + 1) * 128] = lo

    def fac_task(m):
        arrived(SIBLING + m, frecv.at[m, 1 - core])
        decode_factor(m, 1 - core)

    def block_of(i):
        return pl.ds(pl.multiple_of((i % 4) * 128, 128), 128)

    def spread_over(send_ref, recv_ref, out, into, d, device):
        remote(send_ref, recv_ref.at[d - 1], out, into, device).start()

    def over_x(d):
        return at(((x + 4 - d) % 4) * 4 + y, col)

    def over_y(d):
        return at(x * 4 + (y + 4 - d) % 4, col)

    def put(n, q, v):
        vown[n, q] = v
        encode(vsend.at[n, q], v)
        for d in (2, 1, 3):
            spread_over(vsend.at[n, q], vrecv.at[n, q], GATHER_OUT, GATHER + n * Q + q, d, over_x(d))

    def coupling_task():
        loads[1].wait()
        encode(csend, fin[1])
        for d in (2, 1, 3):
            spread_over(csend, crecv, C_OUT, GATHER_C, d, over_x(d))

    def kernel_columns(panel, p):
        inner = lax.dot_general(
            desc[panel], cand[:, p * PAIR:(p + 1) * PAIR], (((0,), (0,)), ((), ())),
            preferred_element_type=F32)
        return inner * inner

    def k_task(panel, p):
        if panel == 0:
            if p == 0:
                loads[3].wait()
            loads[4 + p].wait()
        value = kernel_columns(panel, p)
        for i in range(2):
            put(panel, 2 * p + i, value[:, i * CH:(i + 1) * CH])

    def fill(g, own, recv):
        hi, lo = split(own)
        gbuf[g, block_of(x), 0:CH] = hi
        gbuf[g, block_of(x), CH:PAIR] = lo
        for d in (1, 2, 3):
            hi, lo = split(decode(recv.at[d - 1])[0])
            gbuf[g, block_of(x + d), 0:CH] = hi
            gbuf[g, block_of(x + d), CH:PAIR] = lo

    def product(m, g, rows):
        both = jnp.dot(fbuf[m, 0, rows, :], gbuf[g], preferred_element_type=F32)
        low = jnp.dot(fbuf[m, 1, rows, :], gbuf[g, :, 0:CH], preferred_element_type=F32)
        return both[:, 0:CH] + (both[:, CH:PAIR] + low)

    def scatter(send_ref, recv_ref, out, into):
        for d in (2, 1, 3):
            encode(send_ref.at[d - 1], ptmp[block_of(y + 4 - d), :])
            spread_over(send_ref.at[d - 1], recv_ref, out, into, d, over_y(d))

    def collect(own, recv):
        value = own
        for d in (1, 2, 3):
            value = value + decode(recv.at[d - 1])[0]
        return value

    halves = (slice(0, 256), slice(256, 512))

    def ct_task():
        arrived(GATHER_C, crecv)
        fill(0, fin[1], crecv)
        for rows in halves:
            ptmp[rows, :] = product(2, 0, rows)
        scatter(tsend, trecv, T_OUT, SCATTER_T)
        town[...] = ptmp[block_of(y), :]

    def et_task():
        arrived(SCATTER_T, trecv)
        encode(fmsg.at[1], collect(town[...], trecv), jnp.zeros((1, 128), F32))
        fsend_task(1)

    def s_task(q):
        arrived(GATHER + Q + q, vrecv.at[1, q])
        fill(0, vown[1, q], vrecv.at[1, q])
        for rows in halves:
            sk2[q, rows, :] = product(2, 0, rows)

    def c_task(n, q):
        k = 2 * n
        arrived(GATHER + k * Q + q, vrecv.at[k, q])
        fill(0, vown[k, q], vrecv.at[k, q])
        for rows in halves:
            value = product(n, 0, rows)
            ptmp[rows, :] = value if n == 0 else sk2[q, rows, :] - value
        scatter(psend.at[n, q], precv.at[n, q], SCATTER_OUT, SCATTER + n * Q + q)
        pown[n, q] = ptmp[block_of(y), :]

    def e_task(n, q):
        arrived(SCATTER + n * Q + q, precv.at[n, q])
        value = collect(pown[n, q], precv.at[n, q])
        columns = slice(q * CH, (q + 1) * CH)
        if n == 0:
            put(2, q, value)
            pltpu.make_async_copy(vown.at[2, q], first_out.at[:, columns], lsem.at[4 + Q // 2]).start()
            esum[q:q + 1, :] = jnp.sum(value * value, axis=0, keepdims=True)
        else:
            esum[q:q + 1, :] = esum[q:q + 1, :] + jnp.sum(value * value, axis=0, keepdims=True)
            second[q] = value
            pltpu.make_async_copy(second.at[q], second_out.at[:, columns], lsem.at[5 + Q // 2]).start()

    esum[...] = jnp.zeros_like(esum)
    encode_factor(2)
    encode_factor(0)
    pl.semaphore_wait(barrier, len(partners))
    run = {
        "fsend": lambda n, q: fsend_task(n), "sibling": lambda n, q: sibling_task(n),
        "fac": lambda n, q: fac_task(n), "coupling": lambda n, q: coupling_task(),
        "k": k_task, "s": lambda n, q: s_task(q), "ct": lambda n, q: ct_task(), "et": lambda n, q: et_task(),
        "c": c_task, "e": e_task,
    }
    for name, n, q in TASKS:
        run[name](n, q)

    ebuf[pl.ds(row, 1)] = esum[...][None]
    for d in range(1, 16):
        remote(esum, ebuf.at[row], SPREAD_OUT, SPREAD, at((row + d) % 16, col)).start()
    arrived(SPREAD, ebuf.at[pl.ds(0, 15)])
    total = ebuf[0]
    for i in range(1, 16):
        total = total + ebuf[i]
    ex_out[...] = total * (1.0 / (2.0 * B))

    pltpu.make_async_copy(first_out, first_out, lsem.at[4 + Q // 2]).wait()
    pltpu.make_async_copy(second_out, second_out, lsem.at[5 + Q // 2]).wait()
    departed(GATHER_OUT, vrecv)
    departed(SCATTER_OUT, precv)
    departed(C_OUT, crecv)
    departed(T_OUT, trecv)
    departed(SPREAD_OUT, ebuf.at[pl.ds(0, 15)])
    for m in range(3):
        departed(SIBLING_OUT + m, frecv.at[m, core])

        @pl.when(here)
        def _():
            departed(FACTOR_OUT + m, frecv.at[m, 0, pl.ds(0, 7 * ROWS)])

        @pl.when(jnp.logical_not(here))
        def _():
            departed(FACTOR_OUT + m, frecv.at[m, 0])


def finish(first, second, explained, first_out, second_out, explained_out):
    first_out[...] = first[...]
    second_out[...] = second[...]
    for q in range(Q):
        explained_out[q * CH:(q + 1) * CH] = explained[q, :]


def shards(inducing_desc, candidate_desc, first_inverse, coupling, second_inverse):
    hbm = pl.BlockSpec(memory_space=pl.ANY)
    vmem = pl.BlockSpec(memory_space=pltpu.VMEM)
    first, second, explained = pl.pallas_call(
        kernel,
        out_shape=(
            jax.ShapeDtypeStruct((128, Q * CH), F32),
            jax.ShapeDtypeStruct((128, Q * CH), F32),
            jax.ShapeDtypeStruct((8, 128), F32),
        ),
        in_specs=[hbm] * 5,
        out_specs=(hbm, hbm, vmem),
        scratch_shapes=[
            pltpu.VMEM((2, W, 128), BF16),
            pltpu.VMEM((W, Q * CH), BF16),
            pltpu.VMEM((3, 128, 128), F32),
            pltpu.VMEM((3, ROWS, 128), BF16),
            pltpu.VMEM((3, 2, 8 * ROWS, 128), BF16),
            pltpu.VMEM((3, 2, 512, 512), BF16),
            pltpu.VMEM((3, Q, 128, CH), F32),
            pltpu.VMEM((3, Q, ROWS, CH), BF16),
            pltpu.VMEM((3, Q, 3, ROWS, CH), BF16),
            pltpu.VMEM((1, 512, PAIR), BF16),
            pltpu.VMEM((2, Q, 128, CH), F32),
            pltpu.VMEM((512, CH), F32),
            pltpu.VMEM((2, Q, 3, ROWS, CH), BF16),
            pltpu.VMEM((2, Q, 3, ROWS, CH), BF16),
            pltpu.VMEM((ROWS, 128), BF16),
            pltpu.VMEM((3, ROWS, 128), BF16),
            pltpu.VMEM((3, ROWS, 128), BF16),
            pltpu.VMEM((3, ROWS, 128), BF16),
            pltpu.VMEM((128, 128), F32),
            pltpu.VMEM((Q, 512, CH), F32),
            pltpu.VMEM((Q, 128, CH), F32),
            pltpu.VMEM((8, 128), F32),
            pltpu.VMEM((16, 8, 128), F32),
            pltpu.SemaphoreType.DMA((6 + Q // 2,)),
            pltpu.SemaphoreType.DMA((N_SEND,)),
            pltpu.SemaphoreType.DMA((N_RECV,)),
        ],
        compiler_params=pltpu.CompilerParams(
            collective_id=0, has_side_effects=True, vmem_limit_bytes=60 * 1024 * 1024),
    )(inducing_desc, candidate_desc, first_inverse, coupling, second_inverse)
    return pl.pallas_call(
        finish,
        out_shape=(
            jax.ShapeDtypeStruct((128, Q * CH), F32),
            jax.ShapeDtypeStruct((128, Q * CH), F32),
            jax.ShapeDtypeStruct((Q * CH,), F32),
        ),
        in_specs=[vmem] * 3,
        out_specs=(vmem, vmem, vmem),
    )(first, second, explained)


def solution(mesh):
    return jax.shard_map(
        shards,
        mesh=mesh,
        in_specs=(
            P(None, None, "row"),
            P(None, "col"),
            P("row", "col"),
            P("row", "col"),
            P("row", "col"),
        ),
        out_specs=(P("row", "col"), P("row", "col"), P("col")),
        check_vma=False,
    )
```

```python
import jax
import jax.numpy as jnp
from jax import lax
from jax.experimental import pallas as pl
from jax.experimental.pallas import tpu as pltpu
from jax.sharding import PartitionSpec as P

W = 1960
B = 2048
CH = 128
Q = 6
PAIR = 2 * CH
MESH = pl.DeviceIdType.MESH
F32 = jnp.float32
BF16 = jnp.bfloat16

GATHER, SCATTER, FACTOR, SIBLING, SPREAD, GATHER_C, SCATTER_T, N_RECV = 0, 18, 30, 42, 45, 46, 47, 48
GATHER_OUT, SCATTER_OUT, FACTOR_OUT, SIBLING_OUT, SPREAD_OUT, C_OUT, T_OUT, LAST_OUT, N_SEND = 0, 1, 2, 5, 8, 9, 10, 11, 12
ROWS = 144
TINY = 1e-35


def split(v):
    hi = v.astype(BF16)
    lo = (v - hi.astype(F32)).astype(BF16)
    return hi, lo


def codes_of(v, s):
    t = jnp.abs(v) * (250.0 / s)
    e = jnp.floor(t)
    c = jnp.exp2(e - 125.0) * ((t - e) + 1.0)
    return jnp.where(v < 0.0, -c, c).astype(BF16)


def values_of(c, s):
    c = c.astype(F32)
    a = jnp.abs(c)
    e = jnp.floor(jnp.log2(a) + 0.002)
    t = (e + (a * jnp.exp2(-e) + 124.0)) * (s * (1.0 / 250.0))
    return jnp.where(c < 0.0, -t, t)


def encode(ref, v, diagonal=None):
    top = jnp.max(jnp.abs(v), axis=0, keepdims=True)
    s = (top * 1.01 + TINY).astype(BF16).astype(F32)
    ref[0:128, :] = codes_of(v, s)
    tail = jnp.broadcast_to(s, (16, 128))
    if diagonal is not None:
        hi, lo = split(diagonal)
        index = lax.broadcasted_iota(jnp.int32, (16, 128), 0)
        tail = jnp.where(index == 1, hi.astype(F32), jnp.where(index == 2, lo.astype(F32), tail))
    ref[128:144, :] = tail.astype(BF16)


def decode(ref):
    tail = ref[128:144, :].astype(F32)
    return values_of(ref[0:128, :], tail[0:1, :]), tail[1:2, :] + tail[2:3, :]


TASKS = (
    ("fsend", 2, 0), ("fsend", 0, 0), ("coupling", 0, 0), ("k", 0, 0), ("k", 0, 1), ("k", 0, 2), ("k", 1, 0),
    ("k", 1, 1), ("k", 1, 2), ("sibling", 2, 0), ("fac", 2, 0), ("ct", 0, 0), ("sibling", 0, 0), ("et", 0, 0),
    ("fac", 0, 0), ("c", 0, 0), ("c", 0, 1), ("c", 0, 2), ("c", 0, 3), ("c", 0, 4), ("c", 0, 5), ("s", 0, 0),
    ("s", 0, 1), ("s", 0, 2), ("s", 0, 3), ("e", 0, 0), ("s", 0, 4), ("e", 0, 1), ("s", 0, 5), ("e", 0, 2),
    ("sibling", 1, 0), ("e", 0, 3), ("fac", 1, 0), ("c", 1, 0), ("e", 0, 4), ("c", 1, 1), ("e", 0, 5),
    ("c", 1, 2), ("c", 1, 3), ("e", 1, 0), ("c", 1, 4), ("e", 1, 1), ("c", 1, 5), ("e", 1, 2), ("e", 1, 3),
    ("e", 1, 4), ("e", 1, 5),
)


def kernel(desc_hbm, cand_hbm, f_hbm, c_hbm, s_hbm, first_out, second_out, ex_out,
           desc, cand, fin, fmsg, frecv, fbuf, vown, vsend, vrecv, gbuf, pown, ptmp, psend, precv,
           csend, crecv, tsend, trecv, town, sk2, second, esum, ebuf, lsem, ssem, rsem):
    row = lax.axis_index("row")
    col = lax.axis_index("col")
    x, y = row // 4, row % 4
    z, core = col // 2, col % 2

    def at(r, c):
        return {"row": r, "col": c}

    sibling = at(row, z * 2 + 1 - core)
    to_y = 2 * (z % 2) + core
    parity = y % 2

    def remote(src, dst, out, into, device):
        return pltpu.make_async_remote_copy(
            src_ref=src, dst_ref=dst, send_sem=ssem.at[out], recv_sem=rsem.at[into],
            device_id=device, device_id_type=MESH)

    def arrived(into, ref):
        remote(ref, ref, 0, into, sibling).wait_recv()

    def departed(out, ref):
        remote(ref, ref, out, 0, sibling).wait_send()

    barrier = pltpu.get_barrier_semaphore()
    partners = []
    for i in range(4):
        for j in range(2):
            partners.append(at(x * 4 + 2 * j + core, (2 * ((z // 2 + i + 1) % 4) + y // 2) * 2 + parity))
    partners += [at((row + d) % 16, col) for d in range(1, 16)] + [sibling]
    for device in partners:
        pl.semaphore_signal(barrier, inc=1, device_id=device, device_id_type=MESH)

    loads = []
    for m, ref in enumerate((f_hbm, c_hbm, s_hbm)):
        loads.append(pltpu.make_async_copy(ref, fin.at[m], lsem.at[m]))
    loads.append(pltpu.make_async_copy(desc_hbm, desc, lsem.at[3]))
    for p in range(Q // 2):
        columns = pl.ds(p * PAIR, PAIR)
        loads.append(pltpu.make_async_copy(cand_hbm.at[:, columns], cand.at[:, columns], lsem.at[4 + p]))
    for copy in loads:
        copy.start()

    eye = lax.broadcasted_iota(jnp.int32, (128, 128), 0) == lax.broadcasted_iota(jnp.int32, (128, 128), 1)
    on_diagonal = row == col
    def encode_factor(m):
        loads[m].wait()
        block = fin[m]
        taken = eye & on_diagonal
        diagonal = jnp.sum(jnp.where(taken, block, 0.0), axis=0, keepdims=True)
        encode(fmsg.at[m], jnp.where(taken, 0.0, block), diagonal)

    here = (to_y == y) & (core == parity)
    my_slot = pl.ds(pl.multiple_of(((z // 2) * 2 + y // 2) * ROWS, 16), ROWS)

    def fsend_task(m):
        slot = frecv.at[m, parity, my_slot]
        for dz in (4, 3, 5, 2, 6, 1, 7, 0):
            to_z = (z + dz) % 8
            into = FACTOR + 4 * m + (z // 2 + 4 - to_z // 2) % 4
            copy = remote(fmsg.at[m], slot, FACTOR_OUT + m, into, at(x * 4 + to_y, to_z * 2 + parity))
            if dz:
                copy.start()
            else:
                @pl.when(jnp.logical_not(here))
                def _():
                    copy.start()

                @pl.when(here)
                def _():
                    pltpu.make_async_copy(fmsg.at[m], slot, rsem.at[FACTOR + 4 * m]).start()

    def sibling_task(m):
        for k in (2, 1, 3, 0):
            strip = (z // 2 + k) % 4
            got = frecv.at[m, core, pl.ds(pl.multiple_of(strip * (2 * ROWS), 2 * ROWS), 2 * ROWS)]
            arrived(FACTOR + 4 * m + k, got)
            remote(got, got, SIBLING_OUT + m, SIBLING + m, sibling).start()
        decode_factor(m, core)

    def decode_factor(m, p):
        for i in range(4):
            for j in range(2):
                value, diagonal = decode(frecv.at[m, p, pl.ds((2 * i + j) * ROWS, ROWS)])
                if m != 1:
                    value = value + jnp.where(eye, diagonal, 0.0)
                hi, lo = split(value)
                rows = pl.ds(pl.multiple_of(2 * j * 128 + p * 128, 128), 128)
                fbuf[m, 0, rows, i * 128:(i + 1) * 128] = hi
                fbuf[m, 1, rows, i * 128:(i + 1) * 128] = lo

    def fac_task(m):
        arrived(SIBLING + m, frecv.at[m, 1 - core])
        decode_factor(m, 1 - core)

    def block_of(i):
        return pl.ds(pl.multiple_of((i % 4) * 128, 128), 128)

    def spread_over(send_ref, recv_ref, out, into, d, device):
        remote(send_ref, recv_ref.at[d - 1], out, into, device).start()

    def over_x(d):
        return at(((x + 4 - d) % 4) * 4 + y, col)

    def over_y(d):
        return at(x * 4 + (y + 4 - d) % 4, col)

    def put(n, q, v):
        vown[n, q] = v
        encode(vsend.at[n, q], v)
        for d in (2, 1, 3):
            spread_over(vsend.at[n, q], vrecv.at[n, q], GATHER_OUT, GATHER + n * Q + q, d, over_x(d))

    def coupling_task():
        loads[1].wait()
        encode(csend, fin[1])
        for d in (2, 1, 3):
            spread_over(csend, crecv, C_OUT, GATHER_C, d, over_x(d))

    def kernel_columns(panel, p):
        inner = lax.dot_general(
            desc[panel], cand[:, p * PAIR:(p + 1) * PAIR], (((0,), (0,)), ((), ())),
            preferred_element_type=F32)
        return inner * inner

    def k_task(panel, p):
        if panel == 0:
            if p == 0:
                loads[3].wait()
            loads[4 + p].wait()
        value = kernel_columns(panel, p)
        for i in range(2):
            put(panel, 2 * p + i, value[:, i * CH:(i + 1) * CH])

    def fill(g, own, recv):
        hi, lo = split(own)
        gbuf[g, block_of(x), 0:CH] = hi
        gbuf[g, block_of(x), CH:PAIR] = lo
        for d in (1, 2, 3):
            hi, lo = split(decode(recv.at[d - 1])[0])
            gbuf[g, block_of(x + d), 0:CH] = hi
            gbuf[g, block_of(x + d), CH:PAIR] = lo

    def product(m, g, rows):
        both = jnp.dot(fbuf[m, 0, rows, :], gbuf[g], preferred_element_type=F32)
        low = jnp.dot(fbuf[m, 1, rows, :], gbuf[g, :, 0:CH], preferred_element_type=F32)
        return both[:, 0:CH] + (both[:, CH:PAIR] + low)

    def scatter(send_ref, recv_ref, out, into):
        for d in (2, 1, 3):
            encode(send_ref.at[d - 1], ptmp[block_of(y + 4 - d), :])
            spread_over(send_ref.at[d - 1], recv_ref, out, into, d, over_y(d))

    scales = {}

    def scatter_last(q):
        place = q % 3
        rows = ROWS if place == 2 else 128
        for d in (2, 1, 3):
            ref = psend.at[1, q, d - 1]
            v = ptmp[block_of(y + 4 - d), :]
            top = jnp.max(jnp.abs(v), axis=0, keepdims=True)
            scale = (top * 1.01 + TINY).astype(BF16).astype(F32)
            scales[place, d] = scale
            ref[0:128, :] = codes_of(v, scale)
            if place == 2:
                index = lax.broadcasted_iota(jnp.int32, (16, 128), 0)
                tail = jnp.where(index == 0, scales[0, d], jnp.where(index == 1, scales[1, d], scale))
                ref[128:144, :] = tail.astype(BF16)
            remote(psend.at[1, q, d - 1, pl.ds(0, rows)], precv.at[1, q, d - 1, pl.ds(0, rows)],
                   LAST_OUT, SCATTER + Q + q, over_y(d)).start()

    def collect_last(q):
        value = pown[1, q]
        last = q - q % 3 + 2
        for d in (1, 2, 3):
            tail = precv[1, last, d - 1, 128:144, :].astype(F32)
            value = value + values_of(precv[1, q, d - 1, 0:128, :], tail[q % 3:q % 3 + 1, :])
        return value

    def collect(own, recv):
        value = own
        for d in (1, 2, 3):
            value = value + decode(recv.at[d - 1])[0]
        return value

    halves = (slice(0, 256), slice(256, 512))

    def ct_task():
        arrived(GATHER_C, crecv)
        fill(0, fin[1], crecv)
        for rows in halves:
            ptmp[rows, :] = product(2, 0, rows)
        scatter(tsend, trecv, T_OUT, SCATTER_T)
        town[...] = ptmp[block_of(y), :]

    def et_task():
        arrived(SCATTER_T, trecv)
        encode(fmsg.at[1], collect(town[...], trecv), jnp.zeros((1, 128), F32))
        fsend_task(1)

    def s_task(q):
        arrived(GATHER + Q + q, vrecv.at[1, q])
        fill(0, vown[1, q], vrecv.at[1, q])
        for rows in halves:
            sk2[q, rows, :] = product(2, 0, rows)

    def c_task(n, q):
        k = 2 * n
        arrived(GATHER + k * Q + q, vrecv.at[k, q])
        fill(0, vown[k, q], vrecv.at[k, q])
        for rows in halves:
            value = product(n, 0, rows)
            ptmp[rows, :] = value if n == 0 else sk2[q, rows, :] - value
        if n == 0:
            scatter(psend.at[n, q], precv.at[n, q], SCATTER_OUT, SCATTER + n * Q + q)
        else:
            scatter_last(q)
        pown[n, q] = ptmp[block_of(y), :]

    def e_task(n, q):
        if n == 0:
            arrived(SCATTER + q, precv.at[0, q])
            value = collect(pown[0, q], precv.at[0, q])
            put(2, q, value)
            columns = slice(q * CH, (q + 1) * CH)
            pltpu.make_async_copy(vown.at[2, q], first_out.at[:, columns], lsem.at[4 + Q // 2]).start()
            esum[q:q + 1, :] = jnp.sum(value * value, axis=0, keepdims=True)
        elif q % 3 == 2:
            for p in (q - 2, q - 1, q):
                rows = ROWS if p == q else 128
                arrived(SCATTER + Q + p, precv.at[1, p, :, pl.ds(0, rows)])
            for p in (q - 2, q - 1, q):
                value = collect_last(p)
                columns = slice(p * CH, (p + 1) * CH)
                second[p] = value
                pltpu.make_async_copy(second.at[p], second_out.at[:, columns], lsem.at[5 + Q // 2]).start()
                esum[p:p + 1, :] = esum[p:p + 1, :] + jnp.sum(value * value, axis=0, keepdims=True)

    esum[...] = jnp.zeros_like(esum)
    encode_factor(2)
    encode_factor(0)
    pl.semaphore_wait(barrier, len(partners))
    run = {
        "fsend": lambda n, q: fsend_task(n), "sibling": lambda n, q: sibling_task(n),
        "fac": lambda n, q: fac_task(n), "coupling": lambda n, q: coupling_task(),
        "k": k_task, "s": lambda n, q: s_task(q), "ct": lambda n, q: ct_task(), "et": lambda n, q: et_task(),
        "c": c_task, "e": e_task,
    }
    for name, n, q in TASKS:
        run[name](n, q)

    ebuf[pl.ds(row, 1)] = esum[...][None]
    for d in range(1, 16):
        remote(esum, ebuf.at[row], SPREAD_OUT, SPREAD, at((row + d) % 16, col)).start()
    arrived(SPREAD, ebuf.at[pl.ds(0, 15)])
    total = ebuf[0]
    for i in range(1, 16):
        total = total + ebuf[i]
    ex_out[...] = total * (1.0 / (2.0 * B))

    pltpu.make_async_copy(first_out, first_out, lsem.at[4 + Q // 2]).wait()
    pltpu.make_async_copy(second_out, second_out, lsem.at[5 + Q // 2]).wait()
    departed(GATHER_OUT, vrecv)
    departed(SCATTER_OUT, precv.at[0])
    departed(LAST_OUT, sk2.at[:, pl.ds(0, 200)])
    departed(C_OUT, crecv)
    departed(T_OUT, trecv)
    departed(SPREAD_OUT, ebuf.at[pl.ds(0, 15)])
    for m in range(3):
        departed(SIBLING_OUT + m, frecv.at[m, core])

        @pl.when(here)
        def _():
            departed(FACTOR_OUT + m, frecv.at[m, 0, pl.ds(0, 7 * ROWS)])

        @pl.when(jnp.logical_not(here))
        def _():
            departed(FACTOR_OUT + m, frecv.at[m, 0])


def finish(first, second, explained, first_out, second_out, explained_out):
    first_out[...] = first[...]
    second_out[...] = second[...]
    for q in range(Q):
        explained_out[q * CH:(q + 1) * CH] = explained[q, :]


def shards(inducing_desc, candidate_desc, first_inverse, coupling, second_inverse):
    hbm = pl.BlockSpec(memory_space=pl.ANY)
    vmem = pl.BlockSpec(memory_space=pltpu.VMEM)
    first, second, explained = pl.pallas_call(
        kernel,
        out_shape=(
            jax.ShapeDtypeStruct((128, Q * CH), F32),
            jax.ShapeDtypeStruct((128, Q * CH), F32),
            jax.ShapeDtypeStruct((8, 128), F32),
        ),
        in_specs=[hbm] * 5,
        out_specs=(hbm, hbm, vmem),
        scratch_shapes=[
            pltpu.VMEM((2, W, 128), BF16),
            pltpu.VMEM((W, Q * CH), BF16),
            pltpu.VMEM((3, 128, 128), F32),
            pltpu.VMEM((3, ROWS, 128), BF16),
            pltpu.VMEM((3, 2, 8 * ROWS, 128), BF16),
            pltpu.VMEM((3, 2, 512, 512), BF16),
            pltpu.VMEM((3, Q, 128, CH), F32),
            pltpu.VMEM((3, Q, ROWS, CH), BF16),
            pltpu.VMEM((3, Q, 3, ROWS, CH), BF16),
            pltpu.VMEM((1, 512, PAIR), BF16),
            pltpu.VMEM((2, Q, 128, CH), F32),
            pltpu.VMEM((512, CH), F32),
            pltpu.VMEM((2, Q, 3, ROWS, CH), BF16),
            pltpu.VMEM((2, Q, 3, ROWS, CH), BF16),
            pltpu.VMEM((ROWS, 128), BF16),
            pltpu.VMEM((3, ROWS, 128), BF16),
            pltpu.VMEM((3, ROWS, 128), BF16),
            pltpu.VMEM((3, ROWS, 128), BF16),
            pltpu.VMEM((128, 128), F32),
            pltpu.VMEM((Q, 512, CH), F32),
            pltpu.VMEM((Q, 128, CH), F32),
            pltpu.VMEM((8, 128), F32),
            pltpu.VMEM((16, 8, 128), F32),
            pltpu.SemaphoreType.DMA((6 + Q // 2,)),
            pltpu.SemaphoreType.DMA((N_SEND,)),
            pltpu.SemaphoreType.DMA((N_RECV,)),
        ],
        compiler_params=pltpu.CompilerParams(
            collective_id=0, has_side_effects=True, vmem_limit_bytes=60 * 1024 * 1024),
    )(inducing_desc, candidate_desc, first_inverse, coupling, second_inverse)
    return pl.pallas_call(
        finish,
        out_shape=(
            jax.ShapeDtypeStruct((128, Q * CH), F32),
            jax.ShapeDtypeStruct((128, Q * CH), F32),
            jax.ShapeDtypeStruct((Q * CH,), F32),
        ),
        in_specs=[vmem] * 3,
        out_specs=(vmem, vmem, vmem),
    )(first, second, explained)


def solution(mesh):
    return jax.shard_map(
        shards,
        mesh=mesh,
        in_specs=(
            P(None, None, "row"),
            P(None, "col"),
            P("row", "col"),
            P("row", "col"),
            P("row", "col"),
        ),
        out_specs=(P("row", "col"), P("row", "col"), P("col")),
        check_vma=False,
    )
```
